256 devices in a mesh: line: 8 (over x, core), grid: 32 (over z, y).
Axes of the slice: x: 4, y: 4, z: 8, core: 2. Of those that a mesh axis runs over, the one named last changes fastest.
Arguments:
- psi_start: float32 [5, 128, 8192], P(None, 'line', 'grid'), may hold values from -6 to 6
- objective: float32 [5, 128, 8192], P(None, 'line', 'grid'), may hold values from -6 to 6
- stencil: bfloat16 [5, 5, 5, 128, 8192], P(None, None, None, 'line', 'grid'), may hold values from -0.8984375 to 0.8984375
- lower_factor: float32 [5, 5, 128, 8192], P(None, None, 'line', 'grid'), may hold values from -0.02 to 1
- upper_factor: float32 [5, 5, 128, 8192], P(None, None, 'line', 'grid'), may hold values from -0.15 to 1
- fringe_line: int32 [2048], P('grid'), may hold values from 0 to 255
- donor_owner: int32 [16384, 1], P('grid'), may hold values from 0 to 31; in each aligned block of 512 rows (0 to 511, 512 to 1023, ...) at most 32 rows name the same one
- donor_line: int32 [16384], P('grid'), may hold values from 0 to 255
- donor_weight: float32 [128, 16384], P('line', 'grid'), may hold values from 0.05 to 0.25
Outputs:
- adjoint: float32 [5, 128, 8192], P(None, 'line', 'grid')
- residual: float32 [5, 128, 8192], P(None, 'line', 'grid')
The draws below stay inside these ranges and needn't reach their ends.
Inputs may be any that keep to these rules, and one draw needn't show every extreme that they name: `donor_owner`: in the 512 rows of each block no owner is named more than 32 times, and in some blocks one owner is named exactly 32 times.
All inputs are finite; a program needn't handle non-finite values.
Results may differ from the reference program's by a relative error of at most 0.0003.
Values sent between devices are 32-bit elements; how exact they have to be, the bound alone decides.
A program may use at most 64 MiB of HBM per device.

```python
import math
import jax
import jax.numpy as jnp
import numpy as np
from jax import lax

LINES_DEV = 256
ITERS = 2
DONORS = 8
LINE_POINTS = 128
GRID_BLOCKS = 32
ALL_LINES = 8192
FRINGE = 64
ROWS = 512
CAP = 32


def shared_lines(key):
    return jax.random.uniform(key, (5, 1, ALL_LINES))


def banded_blocks(key, slow_mask, fast_lo, fast_hi, off_size):
    random_key_list = jax.random.split(key, 5)
    gap_size = jnp.exp(jax.random.uniform(random_key_list[0], (5, LINE_POINTS, ALL_LINES), jnp.float32, jnp.log(0.003), jnp.log(0.02)))
    fast_rate = jax.random.uniform(random_key_list[1], (5, LINE_POINTS, ALL_LINES), jnp.float32, fast_lo, fast_hi)
    damping_factor = jnp.where(slow_mask, 1.0 - gap_size, fast_rate)
    spike_events = jax.random.uniform(random_key_list[2], (5, LINE_POINTS, ALL_LINES)) < 4.0 / LINE_POINTS
    spike_threshold = jax.random.uniform(random_key_list[3], (5, LINE_POINTS, ALL_LINES), jnp.float32, 0.5, 0.8)
    damping_factor = jnp.where(spike_events, damping_factor * spike_threshold, damping_factor)
    off_diag = jax.random.uniform(random_key_list[4], (5, 5, LINE_POINTS, ALL_LINES), jnp.float32, -off_size, off_size)
    identity = jnp.eye(5, dtype=jnp.float32)[:, :, None, None]
    return off_diag * (1.0 - identity) + identity * damping_factor[None]


def draw_lower_factor(key, part):
    shared = shared_lines(key)
    key = jax.random.fold_in(key, 11)
    slow_share = 0.5
    slow_mask = shared < slow_share
    return banded_blocks(key, slow_mask, 0.3, 0.9, 0.02)


def draw_upper_factor(key, part):
    shared = shared_lines(key)
    key = jax.random.fold_in(key, 23)
    slow_share = 0.5
    slow_mask = shared >= slow_share
    return banded_blocks(key, slow_mask, -0.15, 0.15, 0.02)


def place_ends(values, own_key, low, high):
    longest = values.shape.index(max(values.shape))
    spots = []
    for shift in (0, 1):
        where = [jax.random.randint(jax.random.fold_in(own_key, axis), (), 0, length) for axis, length in enumerate(values.shape)]
        where[longest] = (where[longest] + shift) % values.shape[longest]
        spots.append(tuple(where))
    return values.at[spots[0]].set(low).at[spots[1]].set(high)


def levels(own_key, shape, shards, smallest, high):
    factor_of = 1.0
    for axis_at, shards_of in shards:
        heights = jax.random.uniform(jax.random.fold_in(jax.random.fold_in(own_key, 6), axis_at), (shards_of,), jnp.float32, smallest / len(shards), high / len(shards))
        factor_of = factor_of * jnp.repeat(jnp.exp(heights), shape[axis_at] // shards_of).reshape((-1,) + (1,) * (len(shape) - 1 - axis_at))
    return factor_of


def assign_block(stream_key, own, number, rows, number_of, top, bound, slope):
    order = jax.random.permutation(stream_key, number_of)
    crowded, common = load_shares(number_of, rows * top, bound, slope, True), load_shares(number_of, rows * top, bound, slope, False)
    places = jnp.arange(number_of)

    def named(sizes, turn):
        used = int((sizes > 0).sum())
        fixed = max(1, used // 4)
        passed = fixed + (places - fixed + turn * (used - fixed)) % max(1, number_of - fixed)
        return jnp.zeros((number_of,), jnp.int32).at[order[jnp.where(places < fixed, places, passed)]].set(jnp.asarray(sizes, jnp.int32))

    sizes = jnp.where(number % 4 == 0, named(crowded, number // 4), named(common, number - number // 4 - 1))
    mixed = jax.random.permutation(jax.random.fold_in(own, 3), number_of)
    source_of, sink = mixed[0:number_of // 2 * 2:2], mixed[1:number_of // 2 * 2:2]
    slack = jnp.minimum(sizes[source_of] - 1, bound - sizes[sink]) // 2
    slack = jnp.where((source_of == order[0]) | (sink == order[0]) | (sizes[sink] == 0), 0, jnp.maximum(slack, 0))
    passed = jax.random.randint(jax.random.fold_in(own, 4), (number_of // 2,), 0, 1 << 20) % (slack + 1)
    sizes = sizes.at[source_of].add(-passed).at[sink].add(passed)
    items = jnp.searchsorted(jnp.cumsum(sizes), jnp.arange(rows * top), side="right").astype(jnp.int32)
    listing = items.reshape(top, rows).T
    listing = listing[jax.random.permutation(jax.random.fold_in(own, 1), rows)]
    turn = jax.random.randint(jax.random.fold_in(own, 2), (rows, 1), 0, top)
    return jnp.take_along_axis(listing, (jnp.arange(top)[None, :] + turn) % top, axis=1)


def load_shares(count, total, reach, slope, full):
    weights = [(1 << 20) // math.isqrt(standing ** slope) + 1 for standing in range(1, count + 1)]
    largest = reach if full else min(reach, max(-(-total // count), total * weights[0] // sum(weights)))
    least = 1 if total - largest >= count - 1 else 0
    given, surplus = [largest] + [least] * (count - 1), total - largest - least * (count - 1)
    while surplus > 0:
        candidates = [i for i in range(1, count) if given[i] < largest] or [i for i in range(1, count) if given[i] < reach]
        pool, left = sum([weights[i] for i in candidates]), surplus
        for i in candidates:
            addition = min(reach - given[i], max(1, left * weights[i] // pool), surplus)
            given[i] = given[i] + addition
            surplus = surplus - addition
    return np.array(given)


def centred(stream_key, extent, width, reach, pieces=(), kind=jnp.bfloat16):
    drawn = jax.random.normal(stream_key, extent, jnp.float32) * width
    if len(pieces) > 0:
        drawn = levels(stream_key, extent, pieces, -0.22, 0.18) * drawn
    return jnp.clip(drawn, min=-reach, max=reach).astype(kind)


def setup_inputs(seed: int = 0) -> dict:
    seeds = jax.random.split(jax.random.key(seed), 10)
    psi_start = centred(seeds[0], (5, LINE_POINTS, ALL_LINES), 1.0, 6.0, ((1, 8), (2, 32)), jnp.float32)
    objective = centred(seeds[1], (5, LINE_POINTS, ALL_LINES), 1.0, 6.0, ((1, 8), (2, 32)), jnp.float32)
    stencil = centred(seeds[2], (5, 5, 5, LINE_POINTS, ALL_LINES), 0.15, 0.8984375, ((3, 8), (4, 32)))
    lower_factor = draw_lower_factor(jax.random.fold_in(seeds[9], 71), 0)
    upper_factor = draw_upper_factor(jax.random.fold_in(seeds[9], 71), 0)
    fringe_line = place_ends(jax.random.randint(seeds[5], (GRID_BLOCKS * FRINGE,), 0, LINES_DEV), jax.random.fold_in(seeds[5], 1), 0, LINES_DEV - 1).astype(jnp.int32)
    donor_owner_keys = jax.random.split(jax.random.fold_in(seeds[6], 1), (GRID_BLOCKS * ROWS) // ROWS)
    donor_owner_turns = jax.random.permutation(jax.random.fold_in(seeds[6], 3), (GRID_BLOCKS * ROWS) // ROWS)
    donor_owner = jax.vmap(lambda own, number: assign_block(jax.random.fold_in(seeds[6], 2), own, number, ROWS, GRID_BLOCKS, 1, CAP, 2))(donor_owner_keys, donor_owner_turns).reshape((GRID_BLOCKS * ROWS, 1))
    donor_line = place_ends(jax.random.randint(seeds[7], (GRID_BLOCKS * ROWS,), 0, LINES_DEV), jax.random.fold_in(seeds[7], 1), 0, LINES_DEV - 1).astype(jnp.int32)
    donor_weight = jnp.clip(0.05 + 0.2 * jax.random.uniform(seeds[8], (LINE_POINTS, GRID_BLOCKS * ROWS), jnp.float32) ** levels(seeds[8], (LINE_POINTS, GRID_BLOCKS * ROWS), ((0, 8), (1, 32)), -0.2, 0.2), 0.05, 0.25)
    return dict(psi_start=psi_start, objective=objective, stencil=stencil, lower_factor=lower_factor, upper_factor=upper_factor, fringe_line=fringe_line, donor_owner=donor_owner, donor_line=donor_line, donor_weight=donor_weight)


relaxation = 0.1
highest = lax.Precision.HIGHEST


def transposed_stencil(adjoint, stencil):
    result = adjoint
    for offset in range(5):
        product = jnp.einsum('ijpl,ipl->jpl', stencil[offset], adjoint, precision=highest)
        if offset == 0:
            result = result + product
        elif offset == 1:
            result = result + jnp.pad(product[:, :-1], ((0, 0), (1, 0), (0, 0)))
        elif offset == 2:
            result = result + jnp.pad(product[:, 1:], ((0, 0), (0, 1), (0, 0)))
        else:
            blocked = product.reshape(product.shape[0], product.shape[1], GRID_BLOCKS, LINES_DEV)
            if offset == 3:
                shifted = jnp.pad(blocked[..., :-1], ((0, 0), (0, 0), (0, 0), (1, 0)))
            else:
                shifted = jnp.pad(blocked[..., 1:], ((0, 0), (0, 0), (0, 0), (0, 1)))
            result = result + shifted.reshape(product.shape)
    return result


def line_chain(matrices, vectors, backward):
    def advance(carried, members):
        matrix, vector = members
        advanced = jnp.einsum('ijl,jl->il', matrix, carried, precision=highest) + vector
        return advanced, advanced

    initial = jnp.zeros(vectors[:, 0].shape, jnp.float32)
    _, stacked = lax.scan(advance, initial, (jnp.moveaxis(matrices, 2, 0), jnp.moveaxis(vectors, 1, 0)), reverse=backward)
    return jnp.moveaxis(stacked, 0, 1)


def reference(psi_start, objective, stencil, lower_factor, upper_factor, fringe_line, donor_owner, donor_line, donor_weight):
    block_of_row = jnp.arange(GRID_BLOCKS * ROWS, dtype=jnp.int32) // ROWS
    source = block_of_row * LINES_DEV + jnp.repeat(fringe_line, DONORS)
    target = donor_owner[:, 0] * LINES_DEV + donor_line
    adjoint = psi_start
    residual = jnp.zeros_like(psi_start)
    for iteration in range(ITERS):
        contrib = adjoint[:, :, source] * donor_weight[None]
        fringe = jnp.zeros_like(adjoint).at[:, :, target].add(contrib)
        residual = objective - transposed_stencil(adjoint, stencil) - fringe
        lowered = line_chain(lower_factor, residual, False)
        update = line_chain(upper_factor, lowered, True)
        adjoint = adjoint + relaxation * update
    return adjoint, residual
```

```python
import jax
import jax.numpy as jnp
from jax import lax
from jax.experimental import pallas as pl
from jax.experimental.pallas import tpu as pltpu
from jax.sharding import PartitionSpec as P

MESH = pl.DeviceIdType.MESH
ITERS = 2
NV = 5
NP = 16
NL = 256
NZ = 8
NY = 4
ND = 8
CAP = 32
ROWS = 512
FRINGE = 64
relaxation = 0.1
f32 = jnp.float32
bf16 = jnp.bfloat16
i32 = jnp.int32


def split(value):
    high = value.astype(bf16)
    low = (value - high.astype(f32)).astype(bf16)
    return high, low


def stacked(value):
    high, low = split(value)
    return jnp.concatenate([high, low], axis=0)


def iota(shape, dim):
    return lax.broadcasted_iota(i32, shape, dim)


def one_hot(mask):
    return jnp.where(mask, 1.0, 0.0).astype(bf16)


def shifted(value, stride, forward, filler):
    points = iota(value.shape, value.ndim - 2)
    if forward:
        return jnp.where(points >= stride, pltpu.roll(value, stride, value.ndim - 2), filler)
    return jnp.where(points < NP - stride, pltpu.roll(value, NP - stride, value.ndim - 2), filler)


def next_level(src, dst, stride, forward):
    @pl.loop(0, 2)
    def _(half):
        lanes = pl.ds(pl.multiple_of(half * 128, 128), 128)
        moved = [
            [shifted(src[k, j, :, lanes], stride, forward, 1.0 if k == j else 0.0) for j in range(NV)]
            for k in range(NV)
        ]
        for i in range(NV):
            row = [src[i, k, :, lanes] for k in range(NV)]
            for j in range(NV):
                total = row[0] * moved[0][j]
                for k in range(1, NV):
                    total = total + row[k] * moved[k][j]
                dst[i, j, :, lanes] = total


def sweep(vectors, levels, forward):
    for stride, matrix in levels:
        moved = [shifted(v, stride, forward, 0.0) for v in vectors]
        result = []
        for i in range(NV):
            total = vectors[i]
            for j in range(NV):
                total = total + matrix[i, j] * moved[j]
            result.append(total)
        vectors = result
    return vectors


def edge_product(block, first, vector):
    total = None
    for j in range(NV):
        term = block[(first + j) * 8 : (first + j) * 8 + 8, :] * vector[j : j + 1, :]
        total = term if total is None else total + term
    return total


def kernel(
    psi, objective, fringe_line, owner, donor_line, weight, stencil_hbm, lower_hbm, upper_hbm,
    adjoint_out, residual_out,
    stencil, lower, upper, low2, low4, low8, low_all, up2, up4, up8, up_all, up_low,
    gather_hot, mid_hot, line_hot, mid_weight,
    zsend0, zrecv0, zsend1, zrecv1, ysend, yrecv, own_sum,
    edge_mats, edges, rim_send, rim_recv, adjoint, base,
    load_sem, zs, zr, ys, yr, ls, lr, ms, mr, rs, rr,
):
    me = lax.axis_index("line")
    grid = lax.axis_index("grid")
    z = lax.div(grid, NY)
    y = lax.rem(grid, NY)

    barrier = pltpu.get_barrier_semaphore()
    z_peer = [None] + [{"grid": lax.rem(z + k, NZ) * NY + y} for k in range(1, NZ)]
    y_peer = [None] + [{"grid": z * NY + lax.rem(y + k, NY)} for k in range(1, NY)]
    l_peer = [None] + [{"line": lax.rem(me + k, ND)} for k in range(1, ND)]
    peers = z_peer[1:] + y_peer[1:] + l_peer[1:]
    for peer in peers:
        pl.semaphore_signal(barrier, inc=1, device_id=peer, device_id_type=MESH)
    loads = [
        pltpu.make_async_copy(src, dst, load_sem.at[n])
        for n, (src, dst) in enumerate([(lower_hbm, lower), (upper_hbm, upper), (stencil_hbm, stencil)])
    ]
    for load in loads:
        load.start()

    def remote(src, dst, send, recv, peer):
        return pltpu.make_async_remote_copy(
            src_ref=src, dst_ref=dst, send_sem=send, recv_sem=recv, device_id=peer, device_id_type=MESH
        )

    pending = []

    def send(copy):
        copy.start()
        pending.append(copy)

    lines = fringe_line[...]
    lines = jnp.concatenate([lines, lines + NL], axis=1)
    gather_hot[...] = one_hot(iota((2 * NL, 128), 0) == lines)

    def gathered(field):
        flat = field.reshape(NV * NP, NL)
        wide = jnp.concatenate([flat[:40], flat[40:]], axis=1)
        picked = jnp.dot(stacked(wide), gather_hot[...], preferred_element_type=f32)
        return picked[:40] + picked[40:]

    first = gathered(psi[...])
    own = owner[...]
    hot = iota((NZ * NY, ROWS), 0) == own
    before = one_hot(iota((ROWS, ROWS), 0) < iota((ROWS, ROWS), 1))
    count = jnp.dot(one_hot(hot), before, preferred_element_type=f32)
    rank = jnp.sum(jnp.where(hot, count, 0.0), axis=0, keepdims=True).astype(i32)
    own_z = own >> 2
    own_y = own & 3
    slot = own_z * 128 + ((own_y - y + own_z - z) & 3) * CAP + rank
    place = one_hot(iota((NZ * NY * CAP, ROWS), 0) == slot)
    which = iota((16, ROWS), 0)
    misc = jnp.where(
        which == 0, donor_line[...].astype(f32), jnp.where(which == 1, (iota((16, ROWS), 1) >> 3).astype(f32), 0.0)
    )
    entries = jnp.concatenate([stacked(weight[...]), misc.astype(bf16)], axis=0)
    table = lax.dot_general(entries, place, (((1,), (1,)), ((), ())), preferred_element_type=f32)
    for zt in range(NZ):
        lanes = slice(zt * 128, zt * 128 + 128)
        zsend0[zt, 0:40, :] = first
        zsend0[zt, 40:56, :] = table[0:16, lanes] + table[16:32, lanes]
        zsend0[zt, 56:64, :] = table[32:40, lanes]
    zrecv0[0] = zsend0[z]

    pl.semaphore_wait(barrier, len(peers))
    for k in (4, 3, 5, 2, 6, 1, 7):
        send(remote(zsend0.at[lax.rem(z + k, NZ)], zrecv0.at[k], zs.at[0, k], zr.at[0, k], z_peer[k]))

    loads[0].wait()
    loads[1].wait()
    next_level(lower, low2, 1, True)
    next_level(low2, low4, 2, True)
    next_level(low4, low8, 4, True)
    next_level(low8, low_all, 8, True)
    next_level(upper, up2, 1, False)
    next_level(up2, up4, 2, False)
    next_level(up4, up8, 4, False)
    next_level(up8, up_all, 8, False)
    low_levels = [(1, lower), (2, low2), (4, low4), (8, low8)]
    up_levels = [(1, upper), (2, up2), (4, up4), (8, up8)]

    @pl.loop(0, NV)
    def _(column):
        result = sweep([low_all[i, column] for i in range(NV)], up_levels, False)
        for i in range(NV):
            up_low[i, column] = result[i]

    mine = edge_mats.at[me]
    mine[...] = jnp.zeros((120, NL), f32)
    for j in range(NV):
        for i in range(NV):
            mine[j * 8 + i : j * 8 + i + 1, :] = low_all[i, j, NP - 1 : NP, :]
            mine[40 + j * 8 + i : 40 + j * 8 + i + 1, :] = up_all[i, j, 0:1, :]
            mine[80 + j * 8 + i : 80 + j * 8 + i + 1, :] = up_low[i, j, 0:1, :]
    for k in range(1, ND):
        send(remote(mine, mine, ms.at[k], mr.at[me], l_peer[k]))

    loads[2].wait()
    adjoint[...] = psi[...]

    for it in range(ITERS):
        field = [adjoint[i] for i in range(NV)]
        rim_send[it] = jnp.zeros((2, 8, NL), f32)
        points = iota((NP, NL), 0)
        across = iota((NP, NL), 1)
        for j in range(NV):
            prods = []
            for o in range(5):
                total = None
                for i in range(NV):
                    term = stencil[o, i, j].astype(f32) * field[i]
                    total = term if total is None else total + term
                prods.append(total)
            rim_send[it, 0, j : j + 1, :] = prods[1][NP - 1 : NP, :]
            rim_send[it, 1, j : j + 1, :] = prods[2][0:1, :]
            total = field[j] + prods[0]
            total = total + jnp.where(points >= 1, pltpu.roll(prods[1], 1, 0), 0.0)
            total = total + jnp.where(points < NP - 1, pltpu.roll(prods[2], NP - 1, 0), 0.0)
            total = total + jnp.where(across >= 1, pltpu.roll(prods[3], 1, 1), 0.0)
            total = total + jnp.where(across < NL - 1, pltpu.roll(prods[4], NL - 1, 1), 0.0)
            base[j] = objective[j] - total
        rims = [
            remote(rim_send.at[it, 0], rim_recv.at[it, 0], rs.at[it, 0], rr.at[it, 0], l_peer[1]),
            remote(rim_send.at[it, 1], rim_recv.at[it, 1], rs.at[it, 1], rr.at[it, 1], l_peer[ND - 1]),
        ]
        for rim in rims:
            send(rim)

        zrecv = zrecv0 if it == 0 else zrecv1
        parts = [None] * NZ
        for k in (0, 1, 7, 2, 6, 3, 5, 4):
            if k > 0:
                arrived = zrecv0.at[k] if it == 0 else zrecv1.at[k]
                remote(arrived, arrived, zs.at[it, k], zr.at[it, k], z_peer[k]).wait_recv()
            if it == 0:
                from_line = zrecv0[k, 57:58, :].astype(i32)
                from_line = jnp.concatenate([from_line, from_line + FRINGE], axis=1)
                mid_hot[k] = one_hot(iota((128, 256), 0) == from_line)
                mid_weight[k] = zrecv0[k, 40:56, :]
            picked = jnp.dot(stacked(zrecv[k, 0:40, :]), mid_hot[k], preferred_element_type=f32)
            picked = picked[:40] + picked[40:]
            picked = jnp.concatenate([picked[:, :128], picked[:, 128:]], axis=0)
            parts[k] = (picked.reshape(NV, NP, 128) * mid_weight[k][None]).reshape(NV * NP, 128)
        group = iota((1, 128), 1) >> 5

        def chosen(pick, j, half):
            value = pick(4 * half + (-j) % 4)
            for c in range(1, 4):
                value = jnp.where(group == c, pick(4 * half + (c - j) % 4), value)
            return value

        for j in (2, 1, 3, 0):
            if it == 0:
                to_line = jnp.concatenate(
                    [chosen(lambda k: zrecv0[k, 56:57, :], j, half) for half in range(2)], axis=1
                ).astype(i32)
                line_hot[j] = one_hot(iota((NL, 256), 0) == to_line)
            mixed = jnp.concatenate([chosen(lambda k: parts[k], j, half) for half in range(2)], axis=1)
            total = lax.dot_general(
                stacked(mixed), line_hot[j], (((1,), (1,)), ((), ())), preferred_element_type=f32
            )
            total = total[:80] + total[80:]
            if j == 0:
                own_sum[...] = total
            else:
                ysend[it, j - 1] = total
                send(remote(ysend.at[it, j - 1], yrecv.at[it, j - 1], ys.at[it, j], yr.at[it, j], y_peer[j]))

        for rim in rims:
            rim.wait_recv()
        below = jnp.where(me > 0, rim_recv[it, 0], 0.0)
        above = jnp.where(me < ND - 1, rim_recv[it, 1], 0.0)
        for j in range(NV):
            extra = jnp.where(points == 0, below[j : j + 1, :], 0.0)
            extra = extra + jnp.where(points == NP - 1, above[j : j + 1, :], 0.0)
            base[j] = base[j] - extra
        for j in range(1, NY):
            remote(yrecv.at[it, j - 1], yrecv.at[it, j - 1], ys.at[it, j], yr.at[it, j], y_peer[j]).wait_recv()
        fringe = (own_sum[...] + yrecv[it, 0]) + (yrecv[it, 1] + yrecv[it, 2])
        residual = base[...] - fringe.reshape(NV, NP, NL)
        if it == ITERS - 1:
            residual_out[...] = residual

        lowered = sweep([residual[i] for i in range(NV)], low_levels, True)
        raised = sweep(lowered, up_levels, False)
        edge = edges.at[it, me]
        edge[...] = jnp.zeros((16, NL), f32)
        for i in range(NV):
            edge[i : i + 1, :] = lowered[i][NP - 1 : NP, :]
            edge[8 + i : 9 + i, :] = raised[i][0:1, :]
        for k in range(1, ND):
            send(remote(edge, edge, ls.at[it, k], lr.at[it, me], l_peer[k]))
        for k in range(1, ND):
            other = lax.rem(me + k, ND)
            if it == 0:
                remote(edge_mats.at[other], edge_mats.at[other], ms.at[k], mr.at[other], l_peer[k]).wait_recv()
            remote(edges.at[it, other], edges.at[it, other], ls.at[it, k], lr.at[it, other], l_peer[k]).wait_recv()
        incoming = [jnp.zeros((8, NL), f32)]
        for f in range(ND - 1):
            incoming.append(edges[it, f, 0:8, :] + edge_product(edge_mats.at[f], 0, incoming[f]))
        returning = [jnp.zeros((8, NL), f32)] * ND
        for f in range(ND - 1, 0, -1):
            returning[f - 1] = (
                edges[it, f, 8:16, :]
                + edge_product(edge_mats.at[f], 10, incoming[f])
                + edge_product(edge_mats.at[f], 5, returning[f])
            )
        carried, back = incoming[0], returning[0]
        for f in range(1, ND):
            carried = jnp.where(me == f, incoming[f], carried)
            back = jnp.where(me == f, returning[f], back)
        for i in range(NV):
            total = raised[i]
            for j in range(NV):
                total = total + up_low[i, j] * carried[j : j + 1, :]
                total = total + up_all[i, j] * back[j : j + 1, :]
            total = adjoint[i] + relaxation * total
            adjoint[i] = total
            if it == ITERS - 1:
                adjoint_out[i] = total
        if it < ITERS - 1:
            following = gathered(adjoint[...])
            zsend1[...] = following
            zrecv1[0] = following
            for k in (4, 3, 5, 2, 6, 1, 7):
                send(remote(zsend1, zrecv1.at[k], zs.at[1, k], zr.at[1, k], z_peer[k]))

    for copy in pending:
        copy.wait_send()


def local(psi, objective, stencil, lower, upper, fringe_line, owner, donor_line, weight):
    vmem = pl.BlockSpec(memory_space=pltpu.VMEM)
    hbm = pl.BlockSpec(memory_space=pl.ANY)
    field = jax.ShapeDtypeStruct((NV, NP, NL), f32)
    matrix = pltpu.VMEM((NV, NV, NP, NL), f32)
    dma = pltpu.SemaphoreType.DMA
    return pl.pallas_call(
        kernel,
        out_shape=(field, field),
        in_specs=[vmem] * 6 + [hbm] * 3,
        out_specs=(vmem, vmem),
        scratch_shapes=[
            pltpu.VMEM((5, NV, NV, NP, NL), bf16),
            *[matrix] * 11,
            pltpu.VMEM((2 * NL, 128), bf16),
            pltpu.VMEM((NZ, 128, 256), bf16),
            pltpu.VMEM((NY, NL, 256), bf16),
            pltpu.VMEM((NZ, NP, 128), f32),
            pltpu.VMEM((NZ, 64, 128), f32),
            pltpu.VMEM((NZ, 64, 128), f32),
            pltpu.VMEM((40, 128), f32),
            pltpu.VMEM((NZ, 40, 128), f32),
            pltpu.VMEM((ITERS, NY - 1, NV * NP, NL), f32),
            pltpu.VMEM((ITERS, NY - 1, NV * NP, NL), f32),
            pltpu.VMEM((NV * NP, NL), f32),
            pltpu.VMEM((ND, 120, NL), f32),
            pltpu.VMEM((ITERS, ND, 16, NL), f32),
            pltpu.VMEM((ITERS, 2, 8, NL), f32),
            pltpu.VMEM((ITERS, 2, 8, NL), f32),
            pltpu.VMEM((NV, NP, NL), f32),
            pltpu.VMEM((NV, NP, NL), f32),
            dma((3,)),
            dma((ITERS, NZ)), dma((ITERS, NZ)),
            dma((ITERS, NY)), dma((ITERS, NY)),
            dma((ITERS, ND)), dma((ITERS, ND)),
            dma((ND,)), dma((ND,)),
            dma((ITERS, 2)), dma((ITERS, 2)),
        ],
        compiler_params=pltpu.CompilerParams(
            collective_id=0, has_side_effects=True, vmem_limit_bytes=56 * 2**20
        ),
        cost_estimate=pl.CostEstimate(flops=20_000_000, bytes_accessed=4_000_000, transcendentals=0),
        name="smooth",
    )(
        psi, objective, fringe_line.reshape(1, FRINGE), owner.reshape(1, ROWS), donor_line.reshape(1, ROWS), weight,
        stencil, lower, upper,
    )


def solution(mesh):
    in_specs = (
        P(None, "line", "grid"),
        P(None, "line", "grid"),
        P(None, None, None, "line", "grid"),
        P(None, None, "line", "grid"),
        P(None, None, "line", "grid"),
        P("grid"),
        P("grid", None),
        P("grid"),
        P("line", "grid"),
    )
    out_specs = (P(None, "line", "grid"), P(None, "line", "grid"))
    return jax.shard_map(local, mesh=mesh, in_specs=in_specs, out_specs=out_specs, check_vma=False)
```

```python
import jax
import jax.numpy as jnp
from jax import lax
from jax.experimental import pallas as pl
from jax.experimental.pallas import tpu as pltpu
from jax.sharding import PartitionSpec as P

MESH = pl.DeviceIdType.MESH
ITERS = 2
NV = 5
NP = 16
NL = 256
NZ = 8
NY = 4
ND = 8
CAP = 32
ROWS = 512
FRINGE = 64
relaxation = 0.1
f32 = jnp.float32
bf16 = jnp.bfloat16
i32 = jnp.int32


def split(value):
    high = value.astype(bf16)
    low = (value - high.astype(f32)).astype(bf16)
    return high, low


def stacked(value):
    high, low = split(value)
    return jnp.concatenate([high, low], axis=0)


def iota(shape, dim):
    return lax.broadcasted_iota(i32, shape, dim)


def one_hot(mask):
    return jnp.where(mask, 1.0, 0.0).astype(bf16)


def shifted(value, stride, forward, filler):
    points = iota(value.shape, value.ndim - 2)
    if forward:
        return jnp.where(points >= stride, pltpu.roll(value, stride, value.ndim - 2), filler)
    return jnp.where(points < NP - stride, pltpu.roll(value, NP - stride, value.ndim - 2), filler)


def next_level(src, dst, stride, forward):
    @pl.loop(0, 2)
    def _(half):
        lanes = pl.ds(pl.multiple_of(half * 128, 128), 128)
        moved = [
            [shifted(src[k, j, :, lanes], stride, forward, 1.0 if k == j else 0.0) for j in range(NV)]
            for k in range(NV)
        ]
        for i in range(NV):
            row = [src[i, k, :, lanes] for k in range(NV)]
            for j in range(NV):
                total = row[0] * moved[0][j]
                for k in range(1, NV):
                    total = total + row[k] * moved[k][j]
                dst[i, j, :, lanes] = total


def sweep(vectors, levels, forward):
    for stride, matrix in levels:
        moved = [shifted(v, stride, forward, 0.0) for v in vectors]
        result = []
        for i in range(NV):
            total = vectors[i]
            for j in range(NV):
                total = total + matrix[i, j] * moved[j]
            result.append(total)
        vectors = result
    return vectors


def edge_product(block, first, vector):
    total = None
    for j in range(NV):
        term = block[(first + j) * 8 : (first + j) * 8 + 8, :] * vector[j : j + 1, :]
        total = term if total is None else total + term
    return total


def kernel(
    psi_hbm, objective_hbm, fringe_line_hbm, owner_hbm, donor_line_hbm, weight_hbm, stencil_hbm, lower_hbm, upper_hbm,
    adjoint_out, residual_out,
    psi, objective, fringe_line, owner, donor_line, weight, stencil, lower, upper, low2, low4, low8, low_all, up2, up4, up8, up_all, up_low,
    gather_hot, mid_hot, line_hot, mid_weight,
    zsend0, zrecv0, zsend1, zrecv1, ysend, yrecv, own_sum,
    edge_mats, edges, rim_send, rim_recv, adjoint, base,
    load_sem, zs, zr, ys, yr, ls, lr, ms, mr, rs, rr,
):
    me = lax.axis_index("line")
    grid = lax.axis_index("grid")
    z = lax.div(grid, NY)
    y = lax.rem(grid, NY)

    barrier = pltpu.get_barrier_semaphore()
    z_peer = [None] + [{"grid": lax.rem(z + k, NZ) * NY + y} for k in range(1, NZ)]
    y_peer = [None] + [{"grid": z * NY + lax.rem(y + k, NY)} for k in range(1, NY)]
    l_peer = [None] + [{"line": lax.rem(me + k, ND)} for k in range(1, ND)]
    peers = z_peer[1:] + y_peer[1:] + l_peer[1:]
    for peer in peers:
        pl.semaphore_signal(barrier, inc=1, device_id=peer, device_id_type=MESH)
    loads = [
        pltpu.make_async_copy(src, dst, load_sem.at[n])
        for n, (src, dst) in enumerate([
            (fringe_line_hbm, fringe_line), (psi_hbm, psi), (owner_hbm, owner), (donor_line_hbm, donor_line),
            (weight_hbm, weight), (lower_hbm, lower), (upper_hbm, upper), (stencil_hbm, stencil),
            (objective_hbm, objective),
        ])
    ]
    for load in loads:
        load.start()

    def remote(src, dst, send, recv, peer):
        return pltpu.make_async_remote_copy(
            src_ref=src, dst_ref=dst, send_sem=send, recv_sem=recv, device_id=peer, device_id_type=MESH
        )

    pending = []

    def send(copy):
        copy.start()
        pending.append(copy)

    loads[0].wait()
    loads[1].wait()
    lines = fringe_line[...]
    lines = jnp.concatenate([lines, lines + NL], axis=1)
    gather_hot[...] = one_hot(iota((2 * NL, 128), 0) == lines)

    def gathered(field):
        flat = field.reshape(NV * NP, NL)
        wide = jnp.concatenate([flat[:40], flat[40:]], axis=1)
        picked = jnp.dot(stacked(wide), gather_hot[...], preferred_element_type=f32)
        return picked[:40] + picked[40:]

    first = gathered(psi[...])
    for load in loads[2:5]:
        load.wait()
    own = owner[...]
    hot = iota((NZ * NY, ROWS), 0) == own
    before = one_hot(iota((ROWS, ROWS), 0) < iota((ROWS, ROWS), 1))
    count = jnp.dot(one_hot(hot), before, preferred_element_type=f32)
    rank = jnp.sum(jnp.where(hot, count, 0.0), axis=0, keepdims=True).astype(i32)
    own_z = own >> 2
    own_y = own & 3
    slot = own_z * 128 + ((own_y - y + own_z - z) & 3) * CAP + rank
    place = one_hot(iota((NZ * NY * CAP, ROWS), 0) == slot)
    which = iota((16, ROWS), 0)
    misc = jnp.where(
        which == 0, donor_line[...].astype(f32), jnp.where(which == 1, (iota((16, ROWS), 1) >> 3).astype(f32), 0.0)
    )
    entries = jnp.concatenate([stacked(weight[...]), misc.astype(bf16)], axis=0)
    table = lax.dot_general(entries, place, (((1,), (1,)), ((), ())), preferred_element_type=f32)
    for zt in range(NZ):
        lanes = slice(zt * 128, zt * 128 + 128)
        zsend0[zt, 0:40, :] = first
        zsend0[zt, 40:56, :] = table[0:16, lanes] + table[16:32, lanes]
        zsend0[zt, 56:58, :] = table[32:34, lanes]
    zrecv0[0] = zsend0[z]

    pl.semaphore_wait(barrier, len(peers))
    for k in (4, 3, 5, 2, 6, 1, 7):
        send(remote(zsend0.at[lax.rem(z + k, NZ)], zrecv0.at[k], zs.at[0, k], zr.at[0, k], z_peer[k]))

    loads[5].wait()
    loads[6].wait()
    next_level(lower, low2, 1, True)
    next_level(low2, low4, 2, True)
    next_level(low4, low8, 4, True)
    next_level(low8, low_all, 8, True)
    next_level(upper, up2, 1, False)
    next_level(up2, up4, 2, False)
    next_level(up4, up8, 4, False)
    next_level(up8, up_all, 8, False)
    low_levels = [(1, lower), (2, low2), (4, low4), (8, low8)]
    up_levels = [(1, upper), (2, up2), (4, up4), (8, up8)]

    @pl.loop(0, NV)
    def _(column):
        result = sweep([low_all[i, column] for i in range(NV)], up_levels, False)
        for i in range(NV):
            up_low[i, column] = result[i]

    mine = edge_mats.at[me]
    mine[...] = jnp.zeros((120, NL), f32)
    for j in range(NV):
        for i in range(NV):
            mine[j * 8 + i : j * 8 + i + 1, :] = low_all[i, j, NP - 1 : NP, :]
            mine[40 + j * 8 + i : 40 + j * 8 + i + 1, :] = up_all[i, j, 0:1, :]
            mine[80 + j * 8 + i : 80 + j * 8 + i + 1, :] = up_low[i, j, 0:1, :]
    for k in range(1, ND):
        send(remote(mine, mine, ms.at[k], mr.at[me], l_peer[k]))

    loads[7].wait()
    loads[8].wait()
    adjoint[...] = psi[...]

    for it in range(ITERS):
        field = [adjoint[i] for i in range(NV)]
        rim_send[it] = jnp.zeros((2, 8, NL), f32)
        points = iota((NP, NL), 0)
        across = iota((NP, NL), 1)
        for j in range(NV):
            prods = []
            for o in range(5):
                total = None
                for i in range(NV):
                    term = stencil[o, i, j].astype(f32) * field[i]
                    total = term if total is None else total + term
                prods.append(total)
            rim_send[it, 0, j : j + 1, :] = prods[1][NP - 1 : NP, :]
            rim_send[it, 1, j : j + 1, :] = prods[2][0:1, :]
            total = field[j] + prods[0]
            total = total + jnp.where(points >= 1, pltpu.roll(prods[1], 1, 0), 0.0)
            total = total + jnp.where(points < NP - 1, pltpu.roll(prods[2], NP - 1, 0), 0.0)
            total = total + jnp.where(across >= 1, pltpu.roll(prods[3], 1, 1), 0.0)
            total = total + jnp.where(across < NL - 1, pltpu.roll(prods[4], NL - 1, 1), 0.0)
            base[j] = objective[j] - total
        rims = [
            remote(rim_send.at[it, 0], rim_recv.at[it, 0], rs.at[it, 0], rr.at[it, 0], l_peer[1]),
            remote(rim_send.at[it, 1], rim_recv.at[it, 1], rs.at[it, 1], rr.at[it, 1], l_peer[ND - 1]),
        ]
        for rim in rims:
            send(rim)

        zrecv = zrecv0 if it == 0 else zrecv1
        parts = [None] * NZ
        for k in (0, 1, 7, 2, 6, 3, 5, 4):
            if k > 0:
                arrived = zrecv0.at[k] if it == 0 else zrecv1.at[k]
                remote(arrived, arrived, zs.at[it, k], zr.at[it, k], z_peer[k]).wait_recv()
            if it == 0:
                from_line = zrecv0[k, 57:58, :].astype(i32)
                from_line = jnp.concatenate([from_line, from_line + FRINGE], axis=1)
                mid_hot[k] = one_hot(iota((128, 256), 0) == from_line)
                mid_weight[k] = zrecv0[k, 40:56, :]
            picked = jnp.dot(stacked(zrecv[k, 0:40, :]), mid_hot[k], preferred_element_type=f32)
            picked = picked[:40] + picked[40:]
            picked = jnp.concatenate([picked[:, :128], picked[:, 128:]], axis=0)
            parts[k] = (picked.reshape(NV, NP, 128) * mid_weight[k][None]).reshape(NV * NP, 128)
        group = iota((1, 128), 1) >> 5

        def chosen(pick, j, half):
            value = pick(4 * half + (-j) % 4)
            for c in range(1, 4):
                value = jnp.where(group == c, pick(4 * half + (c - j) % 4), value)
            return value

        for j in (2, 1, 3, 0):
            if it == 0:
                to_line = jnp.concatenate(
                    [chosen(lambda k: zrecv0[k, 56:57, :], j, half) for half in range(2)], axis=1
                ).astype(i32)
                line_hot[j] = one_hot(iota((NL, 256), 0) == to_line)
            mixed = jnp.concatenate([chosen(lambda k: parts[k], j, half) for half in range(2)], axis=1)
            total = lax.dot_general(
                stacked(mixed), line_hot[j], (((1,), (1,)), ((), ())), preferred_element_type=f32
            )
            total = total[:80] + total[80:]
            if j == 0:
                own_sum[...] = total
            else:
                ysend[it, j - 1] = total
                send(remote(ysend.at[it, j - 1], yrecv.at[it, j - 1], ys.at[it, j], yr.at[it, j], y_peer[j]))

        for rim in rims:
            rim.wait_recv()
        below = jnp.where(me > 0, rim_recv[it, 0], 0.0)
        above = jnp.where(me < ND - 1, rim_recv[it, 1], 0.0)
        for j in range(NV):
            extra = jnp.where(points == 0, below[j : j + 1, :], 0.0)
            extra = extra + jnp.where(points == NP - 1, above[j : j + 1, :], 0.0)
            base[j] = base[j] - extra
        for j in range(1, NY):
            remote(yrecv.at[it, j - 1], yrecv.at[it, j - 1], ys.at[it, j], yr.at[it, j], y_peer[j]).wait_recv()
        fringe = (own_sum[...] + yrecv[it, 0]) + (yrecv[it, 1] + yrecv[it, 2])
        residual = base[...] - fringe.reshape(NV, NP, NL)
        if it == ITERS - 1:
            residual_out[...] = residual

        lowered = sweep([residual[i] for i in range(NV)], low_levels, True)
        raised = sweep(lowered, up_levels, False)
        edge = edges.at[it, me]
        edge[...] = jnp.zeros((16, NL), f32)
        for i in range(NV):
            edge[i : i + 1, :] = lowered[i][NP - 1 : NP, :]
            edge[8 + i : 9 + i, :] = raised[i][0:1, :]
        for k in range(1, ND):
            send(remote(edge, edge, ls.at[it, k], lr.at[it, me], l_peer[k]))
        for k in range(1, ND):
            other = lax.rem(me + k, ND)
            if it == 0:
                remote(edge_mats.at[other], edge_mats.at[other], ms.at[k], mr.at[other], l_peer[k]).wait_recv()
            remote(edges.at[it, other], edges.at[it, other], ls.at[it, k], lr.at[it, other], l_peer[k]).wait_recv()
        incoming = [jnp.zeros((8, NL), f32)]
        for f in range(ND - 1):
            incoming.append(edges[it, f, 0:8, :] + edge_product(edge_mats.at[f], 0, incoming[f]))
        returning = [jnp.zeros((8, NL), f32)] * ND
        for f in range(ND - 1, 0, -1):
            returning[f - 1] = (
                edges[it, f, 8:16, :]
                + edge_product(edge_mats.at[f], 10, incoming[f])
                + edge_product(edge_mats.at[f], 5, returning[f])
            )
        carried, back = incoming[0], returning[0]
        for f in range(1, ND):
            carried = jnp.where(me == f, incoming[f], carried)
            back = jnp.where(me == f, returning[f], back)
        for i in range(NV):
            total = raised[i]
            for j in range(NV):
                total = total + up_low[i, j] * carried[j : j + 1, :]
                total = total + up_all[i, j] * back[j : j + 1, :]
            total = adjoint[i] + relaxation * total
            adjoint[i] = total
            if it == ITERS - 1:
                adjoint_out[i] = total
        if it < ITERS - 1:
            following = gathered(adjoint[...])
            zsend1[...] = following
            zrecv1[0] = following
            for k in (4, 3, 5, 2, 6, 1, 7):
                send(remote(zsend1, zrecv1.at[k], zs.at[1, k], zr.at[1, k], z_peer[k]))

    for copy in pending:
        copy.wait_send()


def local(psi, objective, stencil, lower, upper, fringe_line, owner, donor_line, weight):
    vmem = pl.BlockSpec(memory_space=pltpu.VMEM)
    hbm = pl.BlockSpec(memory_space=pl.ANY)
    field = pltpu.VMEM((NV, NP, NL), f32)
    matrix = pltpu.VMEM((NV, NV, NP, NL), f32)
    dma = pltpu.SemaphoreType.DMA
    return pl.pallas_call(
        kernel,
        out_shape=(field, field),
        in_specs=[hbm] * 9,
        out_specs=(vmem, vmem),
        scratch_shapes=[
            pltpu.VMEM((NV, NP, NL), f32),
            pltpu.VMEM((NV, NP, NL), f32),
            pltpu.VMEM((1, FRINGE), i32),
            pltpu.VMEM((1, ROWS), i32),
            pltpu.VMEM((1, ROWS), i32),
            pltpu.VMEM((NP, ROWS), f32),
            pltpu.VMEM((5, NV, NV, NP, NL), bf16),
            *[matrix] * 11,
            pltpu.VMEM((2 * NL, 128), bf16),
            pltpu.VMEM((NZ, 128, 256), bf16),
            pltpu.VMEM((NY, NL, 256), bf16),
            pltpu.VMEM((NZ, NP, 128), f32),
            pltpu.VMEM((NZ, 58, 128), f32),
            pltpu.VMEM((NZ, 58, 128), f32),
            pltpu.VMEM((40, 128), f32),
            pltpu.VMEM((NZ, 40, 128), f32),
            pltpu.VMEM((ITERS, NY - 1, NV * NP, NL), f32),
            pltpu.VMEM((ITERS, NY - 1, NV * NP, NL), f32),
            pltpu.VMEM((NV * NP, NL), f32),
            pltpu.VMEM((ND, 120, NL), f32),
            pltpu.VMEM((ITERS, ND, 16, NL), f32),
            pltpu.VMEM((ITERS, 2, 8, NL), f32),
            pltpu.VMEM((ITERS, 2, 8, NL), f32),
            pltpu.VMEM((NV, NP, NL), f32),
            pltpu.VMEM((NV, NP, NL), f32),
            dma((9,)),
            dma((ITERS, NZ)), dma((ITERS, NZ)),
            dma((ITERS, NY)), dma((ITERS, NY)),
            dma((ITERS, ND)), dma((ITERS, ND)),
            dma((ND,)), dma((ND,)),
            dma((ITERS, 2)), dma((ITERS, 2)),
        ],
        compiler_params=pltpu.CompilerParams(
            collective_id=0, has_side_effects=True, vmem_limit_bytes=56 * 2**20
        ),
        cost_estimate=pl.CostEstimate(flops=20_000_000, bytes_accessed=4_000_000, transcendentals=0),
        name="smooth",
    )(
        psi, objective, fringe_line.reshape(1, FRINGE), owner.reshape(1, ROWS), donor_line.reshape(1, ROWS), weight,
        stencil, lower, upper,
    )


def solution(mesh):
    in_specs = (
        P(None, "line", "grid"),
        P(None, "line", "grid"),
        P(None, None, None, "line", "grid"),
        P(None, None, "line", "grid"),
        P(None, None, "line", "grid"),
        P("grid"),
        P("grid", None),
        P("grid"),
        P("line", "grid"),
    )
    out_specs = (P(None, "line", "grid"), P(None, "line", "grid"))
    return jax.shard_map(local, mesh=mesh, in_specs=in_specs, out_specs=out_specs, check_vma=False)
```

```python
import jax
import jax.numpy as jnp
from jax import lax
from jax.experimental import pallas as pl
from jax.experimental.pallas import tpu as pltpu
from jax.sharding import PartitionSpec as P

MESH = pl.DeviceIdType.MESH
ITERS = 2
NV = 5
NP = 16
NL = 256
NZ = 8
NY = 4
ND = 8
CAP = 32
ROWS = 512
FRINGE = 64
relaxation = 0.1
f32 = jnp.float32
bf16 = jnp.bfloat16
i32 = jnp.int32


def split(value):
    high = value.astype(bf16)
    low = (value - high.astype(f32)).astype(bf16)
    return high, low


def stacked(value):
    high, low = split(value)
    return jnp.concatenate([high, low], axis=0)


def iota(shape, dim):
    return lax.broadcasted_iota(i32, shape, dim)


def one_hot(mask):
    return jnp.where(mask, 1.0, 0.0).astype(bf16)


def shifted(value, stride, forward, filler):
    points = iota(value.shape, value.ndim - 2)
    if forward:
        return jnp.where(points >= stride, pltpu.roll(value, stride, value.ndim - 2), filler)
    return jnp.where(points < NP - stride, pltpu.roll(value, NP - stride, value.ndim - 2), filler)


def next_level(src, dst, stride, forward):
    @pl.loop(0, 2)
    def _(half):
        lanes = pl.ds(pl.multiple_of(half * 128, 128), 128)
        moved = [
            [shifted(src[k, j, :, lanes], stride, forward, 1.0 if k == j else 0.0) for j in range(NV)]
            for k in range(NV)
        ]
        for i in range(NV):
            row = [src[i, k, :, lanes] for k in range(NV)]
            for j in range(NV):
                total = row[0] * moved[0][j]
                for k in range(1, NV):
                    total = total + row[k] * moved[k][j]
                dst[i, j, :, lanes] = total


def sweep(vectors, levels, forward):
    for stride, matrix in levels:
        moved = [shifted(v, stride, forward, 0.0) for v in vectors]
        result = []
        for i in range(NV):
            total = vectors[i]
            for j in range(NV):
                total = total + matrix[i, j] * moved[j]
            result.append(total)
        vectors = result
    return vectors


def edge_product(block, first, vector):
    total = None
    for j in range(NV):
        term = block[first + j] * vector[j : j + 1, :]
        total = term if total is None else total + term
    return total


def kernel(
    psi_hbm, objective_hbm, fringe_line_hbm, owner_hbm, donor_line_hbm, weight_hbm, stencil_hbm, lower_hbm, upper_hbm,
    both_out,
    psi, objective, fringe_line, owner, donor_line, weight, stencil, lower, upper, low2, low4, low8, low_all, up2, up4, up8, up_all, up_low,
    gather_hot, mid_hot, line_hot,
    tab_send, tab_recv, zsend, zrecv, ysend, yrecv, own_sum,
    edge_mats, edges, rim_send, rim_recv, adjoint, base,
    load_sem, ts, tr, zs, zr, ys, yr, ls, lr, ms, mr, rs, rr,
):
    me = lax.axis_index("line")
    grid = lax.axis_index("grid")
    z = lax.div(grid, NY)
    y = lax.rem(grid, NY)

    barrier = pltpu.get_barrier_semaphore()
    z_peer = [None] + [{"grid": lax.rem(z + k, NZ) * NY + y} for k in range(1, NZ)]
    y_peer = [None] + [{"grid": z * NY + lax.rem(y + k, NY)} for k in range(1, NY)]
    l_peer = [None] + [{"line": lax.rem(me + k, ND)} for k in range(1, ND)]
    peers = z_peer[1:] + y_peer[1:] + l_peer[1:]
    for peer in peers:
        pl.semaphore_signal(barrier, inc=1, device_id=peer, device_id_type=MESH)
    loads = [
        pltpu.make_async_copy(src, dst, load_sem.at[n])
        for n, (src, dst) in enumerate([
            (fringe_line_hbm, fringe_line), (psi_hbm, psi), (owner_hbm, owner), (donor_line_hbm, donor_line),
            (weight_hbm, weight), (lower_hbm, lower), (upper_hbm, upper), (stencil_hbm, stencil),
            (objective_hbm, objective),
        ])
    ]
    for load in loads:
        load.start()

    def remote(src, dst, send, recv, peer):
        return pltpu.make_async_remote_copy(
            src_ref=src, dst_ref=dst, send_sem=send, recv_sem=recv, device_id=peer, device_id_type=MESH
        )

    pending = []

    def send(copy):
        copy.start()
        pending.append(copy)

    loads[0].wait()
    loads[1].wait()
    lines = fringe_line[...]
    lines = jnp.concatenate([lines, lines + NL], axis=1)
    gather_hot[...] = one_hot(iota((2 * NL, 128), 0) == lines)

    def gathered(field):
        flat = field.reshape(NV * NP, NL)
        wide = jnp.concatenate([flat[:40], flat[40:]], axis=1)
        picked = jnp.dot(stacked(wide), gather_hot[...], preferred_element_type=f32)
        return picked[:40] + picked[40:]

    first = gathered(psi[...])
    for load in loads[2:5]:
        load.wait()
    own = owner[...]
    hot = iota((NZ * NY, ROWS), 0) == own
    before = one_hot(iota((ROWS, ROWS), 0) < iota((ROWS, ROWS), 1))
    count = jnp.dot(one_hot(hot), before, preferred_element_type=f32)
    rank = jnp.sum(jnp.where(hot, count, 0.0), axis=0, keepdims=True).astype(i32)
    own_z = own >> 2
    own_y = own & 3
    slot = own_z * 128 + ((own_y - y + own_z - z) & 3) * CAP + rank
    place = one_hot(iota((NZ * NY * CAP, ROWS), 0) == slot)
    which = iota((16, ROWS), 0)
    misc = jnp.where(
        which == 0, donor_line[...].astype(f32), jnp.where(which == 1, (iota((16, ROWS), 1) >> 3).astype(f32), 0.0)
    )
    entries = jnp.concatenate([stacked(weight[...]), misc.astype(bf16)], axis=0)
    table = lax.dot_general(entries, place, (((1,), (1,)), ((), ())), preferred_element_type=f32)
    for zt in range(NZ):
        lanes = slice(zt * 128, zt * 128 + 128)
        tab_send[zt, 0:16, :] = table[0:16, lanes] + table[16:32, lanes]
        tab_send[zt, 16:18, :] = table[32:34, lanes]
    tab_recv[0] = tab_send[z]
    zsend[0] = first
    zrecv[0, 0] = first

    loads[7].wait()
    loads[8].wait()
    adjoint[...] = psi[...]

    points = iota((NP, NL), 0)
    across = iota((NP, NL), 1)

    def local_part(it):
        field = [adjoint[i] for i in range(NV)]
        for j in range(NV):
            prods = []
            for o in range(5):
                total = None
                for i in range(NV):
                    term = stencil[o, i, j].astype(f32) * field[i]
                    total = term if total is None else total + term
                prods.append(total)
            rim_send[it, 0, j : j + 1, :] = prods[1][NP - 1 : NP, :]
            rim_send[it, 1, j : j + 1, :] = prods[2][0:1, :]
            total = field[j] + prods[0]
            total = total + jnp.where(points >= 1, pltpu.roll(prods[1], 1, 0), 0.0)
            total = total + jnp.where(points < NP - 1, pltpu.roll(prods[2], NP - 1, 0), 0.0)
            total = total + jnp.where(across >= 1, pltpu.roll(prods[3], 1, 1), 0.0)
            total = total + jnp.where(across < NL - 1, pltpu.roll(prods[4], NL - 1, 1), 0.0)
            base[j] = objective[j] - total

    def start_rims(it):
        rims = [
            remote(rim_send.at[it, 0], rim_recv.at[it, 0], rs.at[it, 0], rr.at[it, 0], l_peer[1]),
            remote(rim_send.at[it, 1], rim_recv.at[it, 1], rs.at[it, 1], rr.at[it, 1], l_peer[ND - 1]),
        ]
        for rim in rims:
            send(rim)
        return rims

    local_part(0)
    pl.semaphore_wait(barrier, len(peers))
    for k in (4, 3, 5, 2, 6, 1, 7):
        send(remote(tab_send.at[lax.rem(z + k, NZ)], tab_recv.at[k], ts.at[k], tr.at[k], z_peer[k]))
    for k in (4, 3, 5, 2, 6, 1, 7):
        send(remote(zsend.at[0], zrecv.at[0, k], zs.at[0, k], zr.at[0, k], z_peer[k]))

    rims = start_rims(0)
    loads[5].wait()
    loads[6].wait()
    next_level(lower, low2, 1, True)
    next_level(low2, low4, 2, True)
    next_level(low4, low8, 4, True)
    next_level(low8, low_all, 8, True)
    next_level(upper, up2, 1, False)
    next_level(up2, up4, 2, False)
    next_level(up4, up8, 4, False)
    next_level(up8, up_all, 8, False)
    low_levels = [(1, lower), (2, low2), (4, low4), (8, low8)]
    up_levels = [(1, upper), (2, up2), (4, up4), (8, up8)]

    @pl.loop(0, NV)
    def _(column):
        result = sweep([low_all[i, column] for i in range(NV)], up_levels, False)
        for i in range(NV):
            up_low[i, column] = result[i]

    mine = edge_mats.at[me]
    for j in range(NV):
        for i in range(NV):
            mine[j, i : i + 1, :] = low_all[i, j, NP - 1 : NP, :]
            mine[5 + j, i : i + 1, :] = up_all[i, j, 0:1, :]
            mine[10 + j, i : i + 1, :] = up_low[i, j, 0:1, :]
    for k in range(1, ND):
        send(remote(mine, mine, ms.at[k], mr.at[me], l_peer[k]))

    for it in range(ITERS):
        if it > 0:
            local_part(it)
            rims = start_rims(it)
        group = iota((1, 128), 1) >> 5

        def chosen(pick, j, half):
            value = pick(4 * half + (-j) % 4)
            for c in range(1, 4):
                value = jnp.where(group == c, pick(4 * half + (c - j) % 4), value)
            return value

        if it == 0:
            for k in range(1, NZ):
                remote(tab_recv.at[k], tab_recv.at[k], ts.at[k], tr.at[k], z_peer[k]).wait_recv()
            for k in range(NZ):
                from_line = tab_recv[k, 17:18, :].astype(i32)
                from_line = jnp.concatenate([from_line, from_line + FRINGE], axis=1)
                picks = one_hot(iota((128, 256), 0) == from_line)
                mid_hot[k, 0:128, :] = picks
                mid_hot[k, 128:256, :] = picks
            for j in range(NY):
                to_line = jnp.concatenate(
                    [chosen(lambda k: tab_recv[k, 16:17, :], j, half) for half in range(2)], axis=1
                ).astype(i32)
                line_hot[j] = one_hot(iota((NL, 256), 0) == to_line)
        parts = [None] * NZ
        for k in range(1, NZ):
            remote(zrecv.at[it, k], zrecv.at[it, k], zs.at[it, k], zr.at[it, k], z_peer[k]).wait_recv()
        for k in range(NZ):
            picked = jnp.dot(
                jnp.concatenate(split(zrecv[it, k]), axis=1), mid_hot[k], preferred_element_type=f32
            )
            picked = jnp.concatenate([picked[:, :128], picked[:, 128:]], axis=0)
            parts[k] = (picked.reshape(NV, NP, 128) * tab_recv[k, 0:16, :][None]).reshape(NV * NP, 128)

        for j in (2, 1, 3, 0):
            mixed = jnp.concatenate([chosen(lambda k: parts[k], j, half) for half in range(2)], axis=1)
            total = lax.dot_general(
                stacked(mixed), line_hot[j], (((1,), (1,)), ((), ())), preferred_element_type=f32
            )
            total = total[:80] + total[80:]
            if j == 0:
                own_sum[...] = total
            else:
                ysend[it, j - 1] = total
                send(remote(ysend.at[it, j - 1], yrecv.at[it, j - 1], ys.at[it, j], yr.at[it, j], y_peer[j]))

        for rim in rims:
            rim.wait_recv()
        below = jnp.where(me > 0, rim_recv[it, 0], 0.0)
        above = jnp.where(me < ND - 1, rim_recv[it, 1], 0.0)
        for j in range(NV):
            extra = jnp.where(points == 0, below[j : j + 1, :], 0.0)
            extra = extra + jnp.where(points == NP - 1, above[j : j + 1, :], 0.0)
            base[j] = base[j] - extra
        for j in (3, 1, 2):
            remote(yrecv.at[it, j - 1], yrecv.at[it, j - 1], ys.at[it, j], yr.at[it, j], y_peer[j]).wait_recv()
            if j == 1:
                fringe = own_sum[...] + (yrecv[it, 0] + yrecv[it, 2])
                base[...] = base[...] - fringe.reshape(NV, NP, NL)
        residual = base[...] - yrecv[it, 1].reshape(NV, NP, NL)
        if it == ITERS - 1:
            both_out[1] = residual

        lowered = sweep([residual[i] for i in range(NV)], low_levels, True)
        raised = sweep(lowered, up_levels, False)
        edge = edges.at[it, me]
        for i in range(NV):
            edge[0, i : i + 1, :] = lowered[i][NP - 1 : NP, :]
            edge[1, i : i + 1, :] = raised[i][0:1, :]
        for k in range(1, ND):
            send(remote(edge, edge, ls.at[it, k], lr.at[it, me], l_peer[k]))
        for k in range(1, ND):
            other = lax.rem(me + k, ND)
            if it == 0:
                remote(edge_mats.at[other], edge_mats.at[other], ms.at[k], mr.at[other], l_peer[k]).wait_recv()
            remote(edges.at[it, other], edges.at[it, other], ls.at[it, k], lr.at[it, other], l_peer[k]).wait_recv()
        incoming = [jnp.zeros((NV, NL), f32)]
        for f in range(ND - 1):
            incoming.append(edges[it, f, 0] + edge_product(edge_mats.at[f], 0, incoming[f]))
        returning = [jnp.zeros((NV, NL), f32)] * ND
        for f in range(ND - 1, 0, -1):
            returning[f - 1] = (
                edges[it, f, 1]
                + edge_product(edge_mats.at[f], 10, incoming[f])
                + edge_product(edge_mats.at[f], 5, returning[f])
            )
        carried, back = incoming[0], returning[0]
        for f in range(1, ND):
            carried = jnp.where(me == f, incoming[f], carried)
            back = jnp.where(me == f, returning[f], back)
        for i in range(NV):
            total = raised[i]
            for j in range(NV):
                total = total + up_low[i, j] * carried[j : j + 1, :]
                total = total + up_all[i, j] * back[j : j + 1, :]
            total = adjoint[i] + relaxation * total
            adjoint[i] = total
            if it == ITERS - 1:
                both_out[0, i] = total
        if it < ITERS - 1:
            following = gathered(adjoint[...])
            zsend[1] = following
            zrecv[1, 0] = following
            for k in (4, 3, 5, 2, 6, 1, 7):
                send(remote(zsend.at[1], zrecv.at[1, k], zs.at[1, k], zr.at[1, k], z_peer[k]))

    for copy in pending:
        copy.wait_send()


def local(psi, objective, stencil, lower, upper, fringe_line, owner, donor_line, weight):
    vmem = pl.BlockSpec(memory_space=pltpu.VMEM)
    hbm = pl.BlockSpec(memory_space=pl.ANY)
    field = pltpu.VMEM((2, NV, NP, NL), f32)
    matrix = pltpu.VMEM((NV, NV, NP, NL), f32)
    dma = pltpu.SemaphoreType.DMA
    both = pl.pallas_call(
        kernel,
        out_shape=field,
        in_specs=[hbm] * 9,
        out_specs=vmem,
        scratch_shapes=[
            pltpu.VMEM((NV, NP, NL), f32),
            pltpu.VMEM((NV, NP, NL), f32),
            pltpu.VMEM((1, FRINGE), i32),
            pltpu.VMEM((1, ROWS), i32),
            pltpu.VMEM((1, ROWS), i32),
            pltpu.VMEM((NP, ROWS), f32),
            pltpu.VMEM((5, NV, NV, NP, NL), bf16),
            *[matrix] * 11,
            pltpu.VMEM((2 * NL, 128), bf16),
            pltpu.VMEM((NZ, 256, 256), bf16),
            pltpu.VMEM((NY, NL, 256), bf16),
            pltpu.VMEM((NZ, 18, 128), f32),
            pltpu.VMEM((NZ, 18, 128), f32),
            pltpu.VMEM((ITERS, 40, 128), f32),
            pltpu.VMEM((ITERS, NZ, 40, 128), f32),
            pltpu.VMEM((ITERS, NY - 1, NV * NP, NL), f32),
            pltpu.VMEM((ITERS, NY - 1, NV * NP, NL), f32),
            pltpu.VMEM((NV * NP, NL), f32),
            pltpu.VMEM((ND, 15, NV, NL), f32),
            pltpu.VMEM((ITERS, ND, 2, NV, NL), f32),
            pltpu.VMEM((ITERS, 2, NV, NL), f32),
            pltpu.VMEM((ITERS, 2, NV, NL), f32),
            pltpu.VMEM((NV, NP, NL), f32),
            pltpu.VMEM((NV, NP, NL), f32),
            dma((9,)),
            dma((NZ,)), dma((NZ,)),
            dma((ITERS, NZ)), dma((ITERS, NZ)),
            dma((ITERS, NY)), dma((ITERS, NY)),
            dma((ITERS, ND)), dma((ITERS, ND)),
            dma((ND,)), dma((ND,)),
            dma((ITERS, 2)), dma((ITERS, 2)),
        ],
        compiler_params=pltpu.CompilerParams(
            collective_id=0, has_side_effects=True, vmem_limit_bytes=56 * 2**20
        ),
        cost_estimate=pl.CostEstimate(flops=20_000_000, bytes_accessed=4_000_000, transcendentals=0),
        name="smooth",
    )(
        psi, objective, fringe_line.reshape(1, FRINGE), owner.reshape(1, ROWS), donor_line.reshape(1, ROWS), weight,
        stencil, lower, upper,
    )
    return both[0], both[1]


def solution(mesh):
    in_specs = (
        P(None, "line", "grid"),
        P(None, "line", "grid"),
        P(None, None, None, "line", "grid"),
        P(None, None, "line", "grid"),
        P(None, None, "line", "grid"),
        P("grid"),
        P("grid", None),
        P("grid"),
        P("line", "grid"),
    )
    out_specs = (P(None, "line", "grid"), P(None, "line", "grid"))
    return jax.shard_map(local, mesh=mesh, in_specs=in_specs, out_specs=out_specs, check_vma=False)
```

```python
import jax
import jax.numpy as jnp
from jax import lax
from jax.experimental import pallas as pl
from jax.experimental.pallas import tpu as pltpu
from jax.sharding import PartitionSpec as P

MESH = pl.DeviceIdType.MESH
ITERS = 2
NV = 5
NP = 16
NL = 256
NZ = 8
NY = 4
ND = 8
CAP = 32
ROWS = 512
FRINGE = 64
relaxation = 0.1
f32 = jnp.float32
bf16 = jnp.bfloat16
i32 = jnp.int32


def split(value):
    high = value.astype(bf16)
    low = (value - high.astype(f32)).astype(bf16)
    return high, low


def stacked(value):
    high, low = split(value)
    return jnp.concatenate([high, low], axis=0)


def iota(shape, dim):
    return lax.broadcasted_iota(i32, shape, dim)


def one_hot(mask):
    return jnp.where(mask, 1.0, 0.0).astype(bf16)


def shifted(value, stride, forward, filler):
    points = iota(value.shape, value.ndim - 2)
    if forward:
        return jnp.where(points >= stride, pltpu.roll(value, stride, value.ndim - 2), filler)
    return jnp.where(points < NP - stride, pltpu.roll(value, NP - stride, value.ndim - 2), filler)


def next_level(src, dst, stride, forward):
    @pl.loop(0, 2)
    def _(half):
        lanes = pl.ds(pl.multiple_of(half * 128, 128), 128)
        moved = [
            [shifted(src[k, j, :, lanes], stride, forward, 1.0 if k == j else 0.0) for j in range(NV)]
            for k in range(NV)
        ]
        for i in range(NV):
            row = [src[i, k, :, lanes] for k in range(NV)]
            for j in range(NV):
                total = row[0] * moved[0][j]
                for k in range(1, NV):
                    total = total + row[k] * moved[k][j]
                dst[i, j, :, lanes] = total


def sweep(vectors, levels, forward):
    for stride, matrix in levels:
        moved = [shifted(v, stride, forward, 0.0) for v in vectors]
        result = []
        for i in range(NV):
            total = vectors[i]
            for j in range(NV):
                total = total + matrix[i, j] * moved[j]
            result.append(total)
        vectors = result
    return vectors


def edge_product(block, first, vector):
    total = None
    for j in range(NV):
        term = block[first + j] * vector[j : j + 1, :]
        total = term if total is None else total + term
    return total


def kernel(
    psi_hbm, objective_hbm, fringe_line_hbm, owner_hbm, donor_line_hbm, weight_hbm, stencil_hbm, lower_hbm, upper_hbm,
    both_out,
    psi, objective, fringe_line, owner, donor_line, weight, stencil, lower, upper, low2, low4, low8, low_all, up2, up4, up8, up_all, up_low,
    gather_hot, mid_hot, line_hot,
    tab_send, tab_recv, zsend, zrecv, ysend, yrecv, own_sum,
    edge_mats, edges, rim_send, rim_recv, adjoint, base,
    load_sem, ts, tr, zs, zr, ys, yr, ls, lr, ms, mr, rs, rr,
):
    me = lax.axis_index("line")
    grid = lax.axis_index("grid")
    z = lax.div(grid, NY)
    y = lax.rem(grid, NY)

    barrier = pltpu.get_barrier_semaphore()
    z_peer = [None] + [{"grid": lax.rem(z + k, NZ) * NY + y} for k in range(1, NZ)]
    y_peer = [None] + [{"grid": z * NY + lax.rem(y + k, NY)} for k in range(1, NY)]
    l_peer = [None] + [{"line": lax.rem(me + k, ND)} for k in range(1, ND)]
    peers = z_peer[1:] + y_peer[1:] + l_peer[1:]
    for peer in peers:
        pl.semaphore_signal(barrier, inc=1, device_id=peer, device_id_type=MESH)
    loads = [
        pltpu.make_async_copy(src, dst, load_sem.at[n])
        for n, (src, dst) in enumerate([
            (fringe_line_hbm, fringe_line), (psi_hbm, psi), (owner_hbm, owner), (donor_line_hbm, donor_line),
            (weight_hbm, weight), (lower_hbm, lower), (upper_hbm, upper), (stencil_hbm, stencil),
            (objective_hbm, objective),
        ])
    ]
    for load in loads:
        load.start()

    def remote(src, dst, send, recv, peer):
        return pltpu.make_async_remote_copy(
            src_ref=src, dst_ref=dst, send_sem=send, recv_sem=recv, device_id=peer, device_id_type=MESH
        )

    pending = []

    def send(copy):
        copy.start()
        pending.append(copy)

    loads[0].wait()
    loads[1].wait()
    lines = fringe_line[...]
    lines = jnp.concatenate([lines, lines + NL], axis=1)
    gather_hot[...] = one_hot(iota((2 * NL, 128), 0) == lines)

    def gathered(field):
        flat = field.reshape(NV * NP, NL)
        wide = jnp.concatenate([flat[:40], flat[40:]], axis=1)
        picked = jnp.dot(stacked(wide), gather_hot[...], preferred_element_type=f32)
        return picked[:40] + picked[40:]

    first = gathered(psi[...])
    for load in loads[2:5]:
        load.wait()
    own = owner[...]
    hot = iota((NZ * NY, ROWS), 0) == own
    before = one_hot(iota((ROWS, ROWS), 0) < iota((ROWS, ROWS), 1))
    count = jnp.dot(one_hot(hot), before, preferred_element_type=f32)
    rank = jnp.sum(jnp.where(hot, count, 0.0), axis=0, keepdims=True).astype(i32)
    own_z = own >> 2
    own_y = own & 3
    slot = own_z * 128 + ((own_y - y + own_z - z) & 3) * CAP + rank
    place = one_hot(iota((NZ * NY * CAP, ROWS), 0) == slot)
    which = iota((16, ROWS), 0)
    misc = jnp.where(
        which == 0, donor_line[...].astype(f32), jnp.where(which == 1, (iota((16, ROWS), 1) >> 3).astype(f32), 0.0)
    )
    entries = jnp.concatenate([stacked(weight[...]), misc.astype(bf16)], axis=0)
    table = lax.dot_general(entries, place, (((1,), (1,)), ((), ())), preferred_element_type=f32)
    for zt in range(NZ):
        lanes = slice(zt * 128, zt * 128 + 128)
        tab_send[zt, 0:16, :] = table[0:16, lanes] + table[16:32, lanes]
        tab_send[zt, 16:18, :] = table[32:34, lanes]
    tab_recv[0] = tab_send[z]
    zsend[0] = first
    zrecv[0, 0] = first

    loads[7].wait()
    loads[8].wait()
    adjoint[...] = psi[...]

    points = iota((NP, NL), 0)
    across = iota((NP, NL), 1)

    def local_part(it):
        field = [adjoint[i] for i in range(NV)]
        for j in range(NV):
            prods = []
            for o in range(5):
                total = None
                for i in range(NV):
                    term = stencil[o, i, j].astype(f32) * field[i]
                    total = term if total is None else total + term
                prods.append(total)
            rim_send[it, 0, j : j + 1, :] = prods[1][NP - 1 : NP, :]
            rim_send[it, 1, j : j + 1, :] = prods[2][0:1, :]
            total = field[j] + prods[0]
            total = total + jnp.where(points >= 1, pltpu.roll(prods[1], 1, 0), 0.0)
            total = total + jnp.where(points < NP - 1, pltpu.roll(prods[2], NP - 1, 0), 0.0)
            total = total + jnp.where(across >= 1, pltpu.roll(prods[3], 1, 1), 0.0)
            total = total + jnp.where(across < NL - 1, pltpu.roll(prods[4], NL - 1, 1), 0.0)
            base[j] = objective[j] - total

    def start_rims(it):
        rims = [
            remote(rim_send.at[it, 0], rim_recv.at[it, 0], rs.at[it, 0], rr.at[it, 0], l_peer[1]),
            remote(rim_send.at[it, 1], rim_recv.at[it, 1], rs.at[it, 1], rr.at[it, 1], l_peer[ND - 1]),
        ]
        for rim in rims:
            send(rim)
        return rims

    local_part(0)
    pl.semaphore_wait(barrier, len(peers))
    for k in (4, 3, 5, 2, 6, 1, 7):
        send(remote(tab_send.at[lax.rem(z + k, NZ)], tab_recv.at[k], ts.at[k], tr.at[k], z_peer[k]))
    for k in (4, 3, 5, 2, 6, 1, 7):
        send(remote(zsend.at[0], zrecv.at[0, k], zs.at[0, k], zr.at[0, k], z_peer[k]))

    rims = start_rims(0)
    loads[5].wait()
    loads[6].wait()
    next_level(lower, low2, 1, True)
    next_level(low2, low4, 2, True)
    next_level(low4, low8, 4, True)
    next_level(low8, low_all, 8, True)
    next_level(upper, up2, 1, False)
    next_level(up2, up4, 2, False)
    next_level(up4, up8, 4, False)
    next_level(up8, up_all, 8, False)
    low_levels = [(1, lower), (2, low2), (4, low4), (8, low8)]
    up_levels = [(1, upper), (2, up2), (4, up4), (8, up8)]

    @pl.loop(0, NV)
    def _(column):
        result = sweep([low_all[i, column] for i in range(NV)], up_levels, False)
        for i in range(NV):
            up_low[i, column] = result[i]

    mine = edge_mats.at[me]
    for j in range(NV):
        for i in range(NV):
            mine[j, i : i + 1, :] = low_all[i, j, NP - 1 : NP, :]
            mine[5 + j, i : i + 1, :] = up_all[i, j, 0:1, :]
            mine[10 + j, i : i + 1, :] = up_low[i, j, 0:1, :]
    for k in range(1, ND):
        send(remote(mine, mine, ms.at[k], mr.at[me], l_peer[k]))

    for it in range(ITERS):
        if it > 0:
            local_part(it)
            rims = start_rims(it)
        group = iota((1, 128), 1) >> 5

        def chosen(pick, j, half):
            value = pick(4 * half + (-j) % 4)
            for c in range(1, 4):
                value = jnp.where(group == c, pick(4 * half + (c - j) % 4), value)
            return value

        if it == 0:
            for k in range(1, NZ):
                remote(tab_recv.at[k], tab_recv.at[k], ts.at[k], tr.at[k], z_peer[k]).wait_recv()
            for k in range(NZ):
                from_line = tab_recv[k, 17:18, :].astype(i32)
                from_line = jnp.concatenate([from_line, from_line + FRINGE], axis=1)
                picks = one_hot(iota((128, 256), 0) == from_line)
                mid_hot[k, 0:128, :] = picks
                mid_hot[k, 128:256, :] = picks
            for j in range(NY):
                to_line = jnp.concatenate(
                    [chosen(lambda k: tab_recv[k, 16:17, :], j, half) for half in range(2)], axis=1
                ).astype(i32)
                line_hot[j] = one_hot(iota((NL, 256), 0) == to_line)
        parts = [None] * NZ
        for k in range(1, NZ):
            remote(zrecv.at[it, k], zrecv.at[it, k], zs.at[it, k], zr.at[it, k], z_peer[k]).wait_recv()
        for k in range(NZ):
            picked = jnp.dot(
                jnp.concatenate(split(zrecv[it, k]), axis=1), mid_hot[k], preferred_element_type=f32
            )
            picked = jnp.concatenate([picked[:, :128], picked[:, 128:]], axis=0)
            parts[k] = (picked.reshape(NV, NP, 128) * tab_recv[k, 0:16, :][None]).reshape(NV * NP, 128)

        for j in (2, 1, 3, 0):
            mixed = jnp.concatenate([chosen(lambda k: parts[k], j, half) for half in range(2)], axis=1)
            total = lax.dot_general(
                stacked(mixed), line_hot[j], (((1,), (1,)), ((), ())), preferred_element_type=f32
            )
            total = total[:80] + total[80:]
            if j == 0:
                own_sum[...] = total
            else:
                ysend[it, j - 1] = total
                send(remote(ysend.at[it, j - 1], yrecv.at[it, j - 1], ys.at[it, j], yr.at[it, j], y_peer[j]))

        for rim in rims:
            rim.wait_recv()
        below = jnp.where(me > 0, rim_recv[it, 0], 0.0)
        above = jnp.where(me < ND - 1, rim_recv[it, 1], 0.0)
        for j in range(NV):
            extra = jnp.where(points == 0, below[j : j + 1, :], 0.0)
            extra = extra + jnp.where(points == NP - 1, above[j : j + 1, :], 0.0)
            base[j] = base[j] - extra
        for j in (3, 1, 2):
            remote(yrecv.at[it, j - 1], yrecv.at[it, j - 1], ys.at[it, j], yr.at[it, j], y_peer[j]).wait_recv()
            if j == 1:
                fringe = own_sum[...] + (yrecv[it, 0] + yrecv[it, 2])
                base[...] = base[...] - fringe.reshape(NV, NP, NL)
        residual = base[...] - yrecv[it, 1].reshape(NV, NP, NL)
        if it == ITERS - 1:
            both_out[1] = residual

        lowered = sweep([residual[i] for i in range(NV)], low_levels, True)
        raised = sweep(lowered, up_levels, False)
        edge = edges.at[it, me]
        for i in range(NV):
            edge[0, i : i + 1, :] = lowered[i][NP - 1 : NP, :]
            edge[1, i : i + 1, :] = raised[i][0:1, :]
        for k in (1, 7, 2, 6, 3, 5, 4):
            send(remote(edge, edge, ls.at[it, k], lr.at[it, me], l_peer[k]))
        for k in range(1, ND):
            other = lax.rem(me + k, ND)
            if it == 0:
                remote(edge_mats.at[other], edge_mats.at[other], ms.at[k], mr.at[other], l_peer[k]).wait_recv()
            remote(edges.at[it, other], edges.at[it, other], ls.at[it, k], lr.at[it, other], l_peer[k]).wait_recv()
        incoming = [jnp.zeros((NV, NL), f32)]
        for f in range(ND - 1):
            incoming.append(edges[it, f, 0] + edge_product(edge_mats.at[f], 0, incoming[f]))
        returning = [jnp.zeros((NV, NL), f32)] * ND
        for f in range(ND - 1, 0, -1):
            returning[f - 1] = (
                edges[it, f, 1]
                + edge_product(edge_mats.at[f], 10, incoming[f])
                + edge_product(edge_mats.at[f], 5, returning[f])
            )
        carried, back = incoming[0], returning[0]
        for f in range(1, ND):
            carried = jnp.where(me == f, incoming[f], carried)
            back = jnp.where(me == f, returning[f], back)
        for i in range(NV):
            total = raised[i]
            for j in range(NV):
                total = total + up_low[i, j] * carried[j : j + 1, :]
                total = total + up_all[i, j] * back[j : j + 1, :]
            total = adjoint[i] + relaxation * total
            adjoint[i] = total
            if it == ITERS - 1:
                both_out[0, i] = total
        if it < ITERS - 1:
            following = gathered(adjoint[...])
            zsend[1] = following
            zrecv[1, 0] = following
            for k in (4, 3, 5, 2, 6, 1, 7):
                send(remote(zsend.at[1], zrecv.at[1, k], zs.at[1, k], zr.at[1, k], z_peer[k]))

    for copy in pending:
        copy.wait_send()


def local(psi, objective, stencil, lower, upper, fringe_line, owner, donor_line, weight):
    vmem = pl.BlockSpec(memory_space=pltpu.VMEM)
    hbm = pl.BlockSpec(memory_space=pl.ANY)
    field = pltpu.VMEM((2, NV, NP, NL), f32)
    matrix = pltpu.VMEM((NV, NV, NP, NL), f32)
    dma = pltpu.SemaphoreType.DMA
    both = pl.pallas_call(
        kernel,
        out_shape=field,
        in_specs=[hbm] * 9,
        out_specs=vmem,
        scratch_shapes=[
            pltpu.VMEM((NV, NP, NL), f32),
            pltpu.VMEM((NV, NP, NL), f32),
            pltpu.VMEM((1, FRINGE), i32),
            pltpu.VMEM((1, ROWS), i32),
            pltpu.VMEM((1, ROWS), i32),
            pltpu.VMEM((NP, ROWS), f32),
            pltpu.VMEM((5, NV, NV, NP, NL), bf16),
            *[matrix] * 11,
            pltpu.VMEM((2 * NL, 128), bf16),
            pltpu.VMEM((NZ, 256, 256), bf16),
            pltpu.VMEM((NY, NL, 256), bf16),
            pltpu.VMEM((NZ, 18, 128), f32),
            pltpu.VMEM((NZ, 18, 128), f32),
            pltpu.VMEM((ITERS, 40, 128), f32),
            pltpu.VMEM((ITERS, NZ, 40, 128), f32),
            pltpu.VMEM((ITERS, NY - 1, NV * NP, NL), f32),
            pltpu.VMEM((ITERS, NY - 1, NV * NP, NL), f32),
            pltpu.VMEM((NV * NP, NL), f32),
            pltpu.VMEM((ND, 15, NV, NL), f32),
            pltpu.VMEM((ITERS, ND, 2, NV, NL), f32),
            pltpu.VMEM((ITERS, 2, NV, NL), f32),
            pltpu.VMEM((ITERS, 2, NV, NL), f32),
            pltpu.VMEM((NV, NP, NL), f32),
            pltpu.VMEM((NV, NP, NL), f32),
            dma((9,)),
            dma((NZ,)), dma((NZ,)),
            dma((ITERS, NZ)), dma((ITERS, NZ)),
            dma((ITERS, NY)), dma((ITERS, NY)),
            dma((ITERS, ND)), dma((ITERS, ND)),
            dma((ND,)), dma((ND,)),
            dma((ITERS, 2)), dma((ITERS, 2)),
        ],
        compiler_params=pltpu.CompilerParams(
            collective_id=0, has_side_effects=True, vmem_limit_bytes=56 * 2**20
        ),
        cost_estimate=pl.CostEstimate(flops=20_000_000, bytes_accessed=4_000_000, transcendentals=0),
        name="smooth",
    )(
        psi, objective, fringe_line.reshape(1, FRINGE), owner.reshape(1, ROWS), donor_line.reshape(1, ROWS), weight,
        stencil, lower, upper,
    )
    return both[0], both[1]


def solution(mesh):
    in_specs = (
        P(None, "line", "grid"),
        P(None, "line", "grid"),
        P(None, None, None, "line", "grid"),
        P(None, None, "line", "grid"),
        P(None, None, "line", "grid"),
        P("grid"),
        P("grid", None),
        P("grid"),
        P("line", "grid"),
    )
    out_specs = (P(None, "line", "grid"), P(None, "line", "grid"))
    return jax.shard_map(local, mesh=mesh, in_specs=in_specs, out_specs=out_specs, check_vma=False)
```

```python
import jax
import jax.numpy as jnp
from jax import lax
from jax.experimental import pallas as pl
from jax.experimental.pallas import tpu as pltpu
from jax.sharding import PartitionSpec as P

MESH = pl.DeviceIdType.MESH
ITERS = 2
NV = 5
NP = 16
NL = 256
NZ = 8
NY = 4
ND = 8
CAP = 32
ROWS = 512
FRINGE = 64
relaxation = 0.1
f32 = jnp.float32
bf16 = jnp.bfloat16
i32 = jnp.int32


def split(value):
    high = value.astype(bf16)
    low = (value - high.astype(f32)).astype(bf16)
    return high, low


def stacked(value):
    high, low = split(value)
    return jnp.concatenate([high, low], axis=0)


def iota(shape, dim):
    return lax.broadcasted_iota(i32, shape, dim)


def one_hot(mask):
    return jnp.where(mask, 1.0, 0.0).astype(bf16)


def shifted(value, stride, forward, filler):
    points = iota(value.shape, value.ndim - 2)
    if forward:
        return jnp.where(points >= stride, pltpu.roll(value, stride, value.ndim - 2), filler)
    return jnp.where(points < NP - stride, pltpu.roll(value, NP - stride, value.ndim - 2), filler)


def next_level(src, dst, stride, forward):
    @pl.loop(0, 2)
    def _(half):
        lanes = pl.ds(pl.multiple_of(half * 128, 128), 128)
        moved = [
            [shifted(src[k, j, :, lanes], stride, forward, 1.0 if k == j else 0.0) for j in range(NV)]
            for k in range(NV)
        ]
        for i in range(NV):
            row = [src[i, k, :, lanes] for k in range(NV)]
            for j in range(NV):
                total = row[0] * moved[0][j]
                for k in range(1, NV):
                    total = total + row[k] * moved[k][j]
                dst[i, j, :, lanes] = total


def sweep(vectors, levels, forward):
    for stride, matrix in levels:
        moved = [shifted(v, stride, forward, 0.0) for v in vectors]
        result = []
        for i in range(NV):
            total = vectors[i]
            for j in range(NV):
                total = total + matrix[i, j] * moved[j]
            result.append(total)
        vectors = result
    return vectors


def edge_product(block, first, vector):
    total = None
    for j in range(NV):
        term = block[first + j] * vector[j : j + 1, :]
        total = term if total is None else total + term
    return total


def kernel(
    psi_hbm, objective_hbm, fringe_line_hbm, owner_hbm, donor_line_hbm, weight_hbm, stencil_hbm, lower_hbm, upper_hbm,
    both_out,
    psi, objective, fringe_line, owner, donor_line, weight, stencil, lower, upper, low2, low4, low8, low_all, up2, up4, up8, up_all, up_low,
    gather_hot, mid_hot, line_hot,
    tab_send, tab_recv, zsend, zrecv, ysend, yrecv, own_sum,
    edge_mats, edges, rim_send, rim_recv, adjoint, base,
    load_sem, ts, tr, zs, zr, ys, yr, ls, lr, ms, mr, rs, rr,
):
    me = lax.axis_index("line")
    grid = lax.axis_index("grid")
    z = lax.div(grid, NY)
    y = lax.rem(grid, NY)

    barrier = pltpu.get_barrier_semaphore()
    z_peer = [None] + [{"grid": lax.rem(z + k, NZ) * NY + y} for k in range(1, NZ)]
    y_peer = [None] + [{"grid": z * NY + lax.rem(y + k, NY)} for k in range(1, NY)]
    l_peer = [None] + [{"line": lax.rem(me + k, ND)} for k in range(1, ND)]
    peers = z_peer[1:] + y_peer[1:] + l_peer[1:]
    for peer in peers:
        pl.semaphore_signal(barrier, inc=1, device_id=peer, device_id_type=MESH)
    loads = [
        pltpu.make_async_copy(src, dst, load_sem.at[n])
        for n, (src, dst) in enumerate([
            (fringe_line_hbm, fringe_line), (psi_hbm, psi), (owner_hbm, owner), (donor_line_hbm, donor_line),
            (weight_hbm, weight), (lower_hbm, lower), (upper_hbm, upper), (stencil_hbm, stencil),
            (objective_hbm, objective),
        ])
    ]
    for load in loads:
        load.start()

    def remote(src, dst, send, recv, peer):
        return pltpu.make_async_remote_copy(
            src_ref=src, dst_ref=dst, send_sem=send, recv_sem=recv, device_id=peer, device_id_type=MESH
        )

    pending = []

    def send(copy):
        copy.start()
        pending.append(copy)

    loads[0].wait()
    loads[1].wait()
    lines = fringe_line[...]
    lines = jnp.concatenate([lines, lines + NL], axis=1)
    gather_hot[...] = one_hot(iota((2 * NL, 128), 0) == lines)

    def gathered(field):
        flat = field.reshape(NV * NP, NL)
        wide = jnp.concatenate([flat[:40], flat[40:]], axis=1)
        picked = jnp.dot(stacked(wide), gather_hot[...], preferred_element_type=f32)
        return picked[:40] + picked[40:]

    first = gathered(psi[...])
    for load in loads[2:5]:
        load.wait()
    own = owner[...]
    hot = iota((NZ * NY, ROWS), 0) == own
    before = one_hot(iota((ROWS, ROWS), 0) < iota((ROWS, ROWS), 1))
    count = jnp.dot(one_hot(hot), before, preferred_element_type=f32)
    rank = jnp.sum(jnp.where(hot, count, 0.0), axis=0, keepdims=True).astype(i32)
    own_z = own >> 2
    own_y = own & 3
    slot = own_z * 128 + ((own_y - y + own_z - z) & 3) * CAP + rank
    place = one_hot(iota((NZ * NY * CAP, ROWS), 0) == slot)
    which = iota((16, ROWS), 0)
    misc = jnp.where(
        which == 0, donor_line[...].astype(f32), jnp.where(which == 1, (iota((16, ROWS), 1) >> 3).astype(f32), 0.0)
    )
    entries = jnp.concatenate([stacked(weight[...]), misc.astype(bf16)], axis=0)
    table = lax.dot_general(entries, place, (((1,), (1,)), ((), ())), preferred_element_type=f32)
    for zt in range(NZ):
        lanes = slice(zt * 128, zt * 128 + 128)
        tab_send[zt, 0:16, :] = table[0:16, lanes] + table[16:32, lanes]
        tab_send[zt, 16:18, :] = table[32:34, lanes]
    tab_recv[0] = tab_send[z]
    zsend[0] = first
    zrecv[0, 0] = first

    loads[7].wait()
    loads[8].wait()
    adjoint[...] = psi[...]

    points = iota((NP, NL), 0)
    across = iota((NP, NL), 1)

    def local_part(it):
        field = [adjoint[i] for i in range(NV)]
        for j in range(NV):
            prods = []
            for o in range(5):
                total = None
                for i in range(NV):
                    term = stencil[o, i, j].astype(f32) * field[i]
                    total = term if total is None else total + term
                prods.append(total)
            rim_send[it, 0, j : j + 1, :] = prods[1][NP - 1 : NP, :]
            rim_send[it, 1, j : j + 1, :] = prods[2][0:1, :]
            total = field[j] + prods[0]
            total = total + jnp.where(points >= 1, pltpu.roll(prods[1], 1, 0), 0.0)
            total = total + jnp.where(points < NP - 1, pltpu.roll(prods[2], NP - 1, 0), 0.0)
            total = total + jnp.where(across >= 1, pltpu.roll(prods[3], 1, 1), 0.0)
            total = total + jnp.where(across < NL - 1, pltpu.roll(prods[4], NL - 1, 1), 0.0)
            base[j] = objective[j] - total

    def start_rims(it):
        rims = [
            remote(rim_send.at[it, 0], rim_recv.at[it, 0], rs.at[it, 0], rr.at[it, 0], l_peer[1]),
            remote(rim_send.at[it, 1], rim_recv.at[it, 1], rs.at[it, 1], rr.at[it, 1], l_peer[ND - 1]),
        ]
        for rim in rims:
            send(rim)
        return rims

    local_part(0)
    pl.semaphore_wait(barrier, len(peers))
    for k in (4, 3, 5, 2, 6, 1, 7):
        send(remote(tab_send.at[lax.rem(z + k, NZ)], tab_recv.at[k], ts.at[k], tr.at[k], z_peer[k]))
    for k in (4, 3, 5, 2, 6, 1, 7):
        send(remote(zsend.at[0], zrecv.at[0, k], zs.at[0, k], zr.at[0, k], z_peer[k]))

    rims = start_rims(0)
    loads[5].wait()
    loads[6].wait()
    next_level(lower, low2, 1, True)
    next_level(low2, low4, 2, True)
    next_level(low4, low8, 4, True)
    next_level(low8, low_all, 8, True)
    next_level(upper, up2, 1, False)
    next_level(up2, up4, 2, False)
    next_level(up4, up8, 4, False)
    next_level(up8, up_all, 8, False)
    low_levels = [(1, lower), (2, low2), (4, low4), (8, low8)]
    up_levels = [(1, upper), (2, up2), (4, up4), (8, up8)]

    @pl.loop(0, NV)
    def _(column):
        result = sweep([low_all[i, column] for i in range(NV)], up_levels, False)
        for i in range(NV):
            up_low[i, column] = result[i]

    mine = edge_mats.at[me]
    for j in range(NV):
        for i in range(NV):
            mine[j, i : i + 1, :] = low_all[i, j, NP - 1 : NP, :]
            mine[5 + j, i : i + 1, :] = up_all[i, j, 0:1, :]
            mine[10 + j, i : i + 1, :] = up_low[i, j, 0:1, :]
    for k in (1, 7, 2, 6, 3, 5, 4):
        send(remote(mine, mine, ms.at[k], mr.at[me], l_peer[k]))

    for it in range(ITERS):
        if it > 0:
            local_part(it)
            rims = start_rims(it)
        group = iota((1, 128), 1) >> 5

        def chosen(pick, j, half):
            value = pick(4 * half + (-j) % 4)
            for c in range(1, 4):
                value = jnp.where(group == c, pick(4 * half + (c - j) % 4), value)
            return value

        if it == 0:
            for k in range(1, NZ):
                remote(tab_recv.at[k], tab_recv.at[k], ts.at[k], tr.at[k], z_peer[k]).wait_recv()
            for k in range(NZ):
                from_line = tab_recv[k, 17:18, :].astype(i32)
                from_line = jnp.concatenate([from_line, from_line + FRINGE], axis=1)
                picks = one_hot(iota((128, 256), 0) == from_line)
                mid_hot[k, 0:128, :] = picks
                mid_hot[k, 128:256, :] = picks
            for j in range(NY):
                to_line = jnp.concatenate(
                    [chosen(lambda k: tab_recv[k, 16:17, :], j, half) for half in range(2)], axis=1
                ).astype(i32)
                line_hot[j] = one_hot(iota((NL, 256), 0) == to_line)
        parts = [None] * NZ
        for k in range(1, NZ):
            remote(zrecv.at[it, k], zrecv.at[it, k], zs.at[it, k], zr.at[it, k], z_peer[k]).wait_recv()
        for k in range(NZ):
            picked = jnp.dot(
                jnp.concatenate(split(zrecv[it, k]), axis=1), mid_hot[k], preferred_element_type=f32
            )
            picked = jnp.concatenate([picked[:, :128], picked[:, 128:]], axis=0)
            parts[k] = (picked.reshape(NV, NP, 128) * tab_recv[k, 0:16, :][None]).reshape(NV * NP, 128)

        for j in (2, 1, 3, 0):
            mixed = jnp.concatenate([chosen(lambda k: parts[k], j, half) for half in range(2)], axis=1)
            total = lax.dot_general(
                stacked(mixed), line_hot[j], (((1,), (1,)), ((), ())), preferred_element_type=f32
            )
            total = total[:80] + total[80:]
            if j == 0:
                own_sum[...] = total
            else:
                ysend[it, j - 1] = total
                send(remote(ysend.at[it, j - 1], yrecv.at[it, j - 1], ys.at[it, j], yr.at[it, j], y_peer[j]))

        for rim in rims:
            rim.wait_recv()
        below = jnp.where(me > 0, rim_recv[it, 0], 0.0)
        above = jnp.where(me < ND - 1, rim_recv[it, 1], 0.0)
        for j in range(NV):
            extra = jnp.where(points == 0, below[j : j + 1, :], 0.0)
            extra = extra + jnp.where(points == NP - 1, above[j : j + 1, :], 0.0)
            base[j] = base[j] - extra
        for j in (3, 1, 2):
            remote(yrecv.at[it, j - 1], yrecv.at[it, j - 1], ys.at[it, j], yr.at[it, j], y_peer[j]).wait_recv()
            if j == 1:
                fringe = own_sum[...] + (yrecv[it, 0] + yrecv[it, 2])
                base[...] = base[...] - fringe.reshape(NV, NP, NL)
        residual = base[...] - yrecv[it, 1].reshape(NV, NP, NL)
        if it == ITERS - 1:
            both_out[1] = residual

        lowered = sweep([residual[i] for i in range(NV)], low_levels, True)
        raised = sweep(lowered, up_levels, False)
        edge = edges.at[it, me]
        for i in range(NV):
            edge[0, i : i + 1, :] = lowered[i][NP - 1 : NP, :]
            edge[1, i : i + 1, :] = raised[i][0:1, :]
        for k in (1, 7, 2, 6, 3, 5, 4):
            send(remote(edge, edge, ls.at[it, k], lr.at[it, me], l_peer[k]))
        for k in range(1, ND):
            other = lax.rem(me + k, ND)
            if it == 0:
                remote(edge_mats.at[other], edge_mats.at[other], ms.at[k], mr.at[other], l_peer[k]).wait_recv()
            remote(edges.at[it, other], edges.at[it, other], ls.at[it, k], lr.at[it, other], l_peer[k]).wait_recv()
        incoming = [jnp.zeros((NV, NL), f32)]
        for f in range(ND - 1):
            incoming.append(edges[it, f, 0] + edge_product(edge_mats.at[f], 0, incoming[f]))
        returning = [jnp.zeros((NV, NL), f32)] * ND
        for f in range(ND - 1, 0, -1):
            returning[f - 1] = (
                edges[it, f, 1]
                + edge_product(edge_mats.at[f], 10, incoming[f])
                + edge_product(edge_mats.at[f], 5, returning[f])
            )
        carried, back = incoming[0], returning[0]
        for f in range(1, ND):
            carried = jnp.where(me == f, incoming[f], carried)
            back = jnp.where(me == f, returning[f], back)
        for i in range(NV):
            total = raised[i]
            for j in range(NV):
                total = total + up_low[i, j] * carried[j : j + 1, :]
                total = total + up_all[i, j] * back[j : j + 1, :]
            total = adjoint[i] + relaxation * total
            adjoint[i] = total
            if it == ITERS - 1:
                both_out[0, i] = total
        if it < ITERS - 1:
            following = gathered(adjoint[...])
            zsend[1] = following
            zrecv[1, 0] = following
            for k in (3, 4, 5, 2, 6, 1, 7):
                send(remote(zsend.at[1], zrecv.at[1, k], zs.at[1, k], zr.at[1, k], z_peer[k]))

    for copy in pending:
        copy.wait_send()


def local(psi, objective, stencil, lower, upper, fringe_line, owner, donor_line, weight):
    vmem = pl.BlockSpec(memory_space=pltpu.VMEM)
    hbm = pl.BlockSpec(memory_space=pl.ANY)
    field = pltpu.VMEM((2, NV, NP, NL), f32)
    matrix = pltpu.VMEM((NV, NV, NP, NL), f32)
    dma = pltpu.SemaphoreType.DMA
    both = pl.pallas_call(
        kernel,
        out_shape=field,
        in_specs=[hbm] * 9,
        out_specs=vmem,
        scratch_shapes=[
            pltpu.VMEM((NV, NP, NL), f32),
            pltpu.VMEM((NV, NP, NL), f32),
            pltpu.VMEM((1, FRINGE), i32),
            pltpu.VMEM((1, ROWS), i32),
            pltpu.VMEM((1, ROWS), i32),
            pltpu.VMEM((NP, ROWS), f32),
            pltpu.VMEM((5, NV, NV, NP, NL), bf16),
            *[matrix] * 11,
            pltpu.VMEM((2 * NL, 128), bf16),
            pltpu.VMEM((NZ, 256, 256), bf16),
            pltpu.VMEM((NY, NL, 256), bf16),
            pltpu.VMEM((NZ, 18, 128), f32),
            pltpu.VMEM((NZ, 18, 128), f32),
            pltpu.VMEM((ITERS, 40, 128), f32),
            pltpu.VMEM((ITERS, NZ, 40, 128), f32),
            pltpu.VMEM((ITERS, NY - 1, NV * NP, NL), f32),
            pltpu.VMEM((ITERS, NY - 1, NV * NP, NL), f32),
            pltpu.VMEM((NV * NP, NL), f32),
            pltpu.VMEM((ND, 15, NV, NL), f32),
            pltpu.VMEM((ITERS, ND, 2, NV, NL), f32),
            pltpu.VMEM((ITERS, 2, NV, NL), f32),
            pltpu.VMEM((ITERS, 2, NV, NL), f32),
            pltpu.VMEM((NV, NP, NL), f32),
            pltpu.VMEM((NV, NP, NL), f32),
            dma((9,)),
            dma((NZ,)), dma((NZ,)),
            dma((ITERS, NZ)), dma((ITERS, NZ)),
            dma((ITERS, NY)), dma((ITERS, NY)),
            dma((ITERS, ND)), dma((ITERS, ND)),
            dma((ND,)), dma((ND,)),
            dma((ITERS, 2)), dma((ITERS, 2)),
        ],
        compiler_params=pltpu.CompilerParams(
            collective_id=0, has_side_effects=True, vmem_limit_bytes=56 * 2**20
        ),
        cost_estimate=pl.CostEstimate(flops=20_000_000, bytes_accessed=4_000_000, transcendentals=0),
        name="smooth",
    )(
        psi, objective, fringe_line.reshape(1, FRINGE), owner.reshape(1, ROWS), donor_line.reshape(1, ROWS), weight,
        stencil, lower, upper,
    )
    return both[0], both[1]


def solution(mesh):
    in_specs = (
        P(None, "line", "grid"),
        P(None, "line", "grid"),
        P(None, None, None, "line", "grid"),
        P(None, None, "line", "grid"),
        P(None, None, "line", "grid"),
        P("grid"),
        P("grid", None),
        P("grid"),
        P("line", "grid"),
    )
    out_specs = (P(None, "line", "grid"), P(None, "line", "grid"))
    return jax.shard_map(local, mesh=mesh, in_specs=in_specs, out_specs=out_specs, check_vma=False)
```
